512 devices in a mesh: blk: 32 (over x, y_lo, core), uly: 16 (over y_hi, z).
Axes of the slice: x: 4, y: 8 (y_hi: 2, y_lo: 4; y = y_hi * 4 + y_lo), z: 8, core: 2. Of those that a mesh axis runs over, the one named last changes fastest.
Arguments:
- query_in: bfloat16 [65536, 4096], P(('blk', 'uly')), may hold values from -16 to 16, as said below
- key_in: bfloat16 [65536, 2048], P(('blk', 'uly')), may hold values from -16 to 16, as said below
- value_in: bfloat16 [65536, 2048], P(('blk', 'uly')), may hold values from -6 to 6
- grad_out: bfloat16 [65536, 4096], P(('blk', 'uly')), may hold values from -6 to 6
- row_dot: bfloat16 [65536, 16], P(('blk', 'uly')), may hold values from -96 to 96
- segments: int32 [65536], replicated, may hold values from 0 to 15, never falling along the last dimension, each value on 1 to 8192 neighbouring positions
Outputs:
- grad_query: bfloat16 [65536, 4096], P(('blk', 'uly'))
- grad_key: bfloat16 [65536, 2048], P(('blk', 'uly'))
- grad_value: bfloat16 [65536, 2048], P(('blk', 'uly'))
The draws below stay inside these ranges and needn't reach their ends.
Inputs may be any that keep to these rules, and one draw needn't show every extreme that they name: `query_in`: queries: entries of independent magnitude, each token and head with its own scale. `key_in`: keys: entries of independent magnitude, each token and head with its own scale.
All inputs are finite; a program needn't handle non-finite values.
Results may differ from the reference program's by a relative error of at most 0.006.
Values may be sent and summed in bfloat16 or wider, within the bound.
A program may use at most 64 MiB of HBM per device.

```python
import math
import jax
import jax.numpy as jnp
import numpy as np
from jax import lax

HEADS = 16
KV_HEADS = 8
HEAD_DIM = 256
WINDOW = 512
BLOCK = 2048
SEQ = 65536
DOCS = 16
DOC_MOST = 8192


def draw_query_in(key, part):
    key = jax.random.fold_in(key, 11)
    entry_key, scale_key = jax.random.split(key)
    entries = jnp.clip(jax.random.normal(entry_key, (SEQ, HEADS, HEAD_DIM), jnp.float32), -4.0, 4.0)
    spread = jnp.exp(jax.random.uniform(scale_key, (SEQ, HEADS, 1), jnp.float32, math.log(0.4), math.log(4.0)))
    return (entries * spread).reshape(SEQ, HEADS * HEAD_DIM).astype(jnp.bfloat16)


def draw_key_in(key, part):
    key = jax.random.fold_in(key, 12)
    entry_key, scale_key = jax.random.split(key)
    entries = jnp.clip(jax.random.normal(entry_key, (SEQ, KV_HEADS, HEAD_DIM), jnp.float32), -4.0, 4.0)
    spread = jnp.exp(jax.random.uniform(scale_key, (SEQ, KV_HEADS, 1), jnp.float32, math.log(0.4), math.log(4.0)))
    return (entries * spread).reshape(SEQ, KV_HEADS * HEAD_DIM).astype(jnp.bfloat16)


def steps_of(stream_key, extent, shards, least, high):
    gain, own = 1.0, jax.random.fold_in(stream_key, 6)
    for dim, shards_of in shards:
        draws = jnp.exp(jax.random.uniform(jax.random.fold_in(own, dim), (shards_of,), jnp.float32, least / len(shards), high / len(shards)))
        gain = gain * jnp.repeat(draws, extent[dim] // shards_of).reshape([-1 if axis == dim else 1 for axis in range(len(extent))])
    return gain


def length_profile(count, total, most, slope):
    loads = [(1 << 20) // math.isqrt(grade ** slope) + 1 for grade in range(2, count + 1)]
    surplus, counts = total - most - (count - 1), [1] * (count - 1)
    while surplus > 0:
        candidates = [i for i in range(count - 1) if counts[i] < most]
        whole, remaining = sum([loads[i] for i in candidates]), surplus
        for i in candidates:
            more = min(most - counts[i], max(1, remaining * loads[i] // whole), surplus)
            counts[i] = counts[i] + more
            surplus = surplus - more
    return np.array([most] + counts)


def uneven_parts(rng, number_of, total, limit, skew):
    if number_of == 2:
        one = jax.random.randint(rng, (), max(1, total - limit), min(limit, total - 1) + 1)
        return jnp.stack([one, total - one])
    sizes = jnp.asarray(length_profile(number_of, total, limit, skew), jnp.int32)
    twos = (number_of - 1) // 2
    donor, sink = sizes[1:1 + 2 * twos:2], sizes[2:2 + 2 * twos:2]
    room = jnp.minimum(donor - 1, limit - sink)
    moved = jax.random.randint(jax.random.fold_in(rng, 1), (twos,), 0, 1 << 20) % (room + 1)
    sizes = sizes.at[1:1 + 2 * twos:2].set(donor - moved).at[2:2 + 2 * twos:2].set(sink + moved)
    return sizes[jax.random.permutation(jax.random.fold_in(rng, 2), number_of)]


def noise(rng, extent, scale, reach, cuts=(), kind=jnp.bfloat16):
    values = scale * jax.random.normal(rng, extent, jnp.float32)
    if cuts:
        values = values * steps_of(rng, extent, cuts, -0.22, 0.18)
    return jnp.clip(values, -reach, reach).astype(kind)


def setup_inputs(seed: int = 0) -> dict:
    streams_of = jax.random.split(jax.random.key(seed), 7)
    query_in = draw_query_in(jax.random.fold_in(streams_of[6], 71), 0)
    key_in = draw_key_in(jax.random.fold_in(streams_of[6], 71), 0)
    value_in = noise(streams_of[2], (SEQ, KV_HEADS * HEAD_DIM), 1.0, 6.0, ((0, 512),))
    grad_out = noise(streams_of[3], (SEQ, HEADS * HEAD_DIM), 1.0, 6.0, ((0, 512),))
    row_dot = noise(streams_of[4], (SEQ, HEADS), 16.0, 96.0, ((0, 512),))
    segments = jnp.searchsorted(jnp.cumsum(uneven_parts(streams_of[5], DOCS, SEQ, DOC_MOST, 2)), jnp.arange(SEQ), side="right").astype(jnp.int32)
    return {"query_in": query_in, "key_in": key_in, "value_in": value_in, "grad_out": grad_out, "row_dot": row_dot, "segments": segments}


query_scale = 0.0625
soft_cap = 50.0


def round_low(values):
    lowered = values.astype(jnp.bfloat16)
    lowered = lax.optimization_barrier(lowered)
    return lowered.astype(jnp.float32)


def reference(query_in, key_in, value_in, grad_out, row_dot, segments):
    length = query_in.shape[0]
    groups = HEADS // KV_HEADS
    qblock = min(512, BLOCK)
    query_all = query_in.reshape(length, HEADS, HEAD_DIM).astype(jnp.float32)
    key_all = jnp.repeat(key_in.reshape(length, KV_HEADS, HEAD_DIM), groups, axis=1).astype(jnp.float32)
    value_all = jnp.repeat(value_in.reshape(length, KV_HEADS, HEAD_DIM), groups, axis=1).astype(jnp.float32)
    grad_all = grad_out.reshape(length, HEADS, HEAD_DIM).astype(jnp.float32)
    rowsum = row_dot.astype(jnp.float32)
    margin = WINDOW
    zero_rows = jnp.zeros((margin, HEADS, HEAD_DIM), jnp.float32)
    key_pad = jnp.concatenate([zero_rows, key_all], axis=0)
    value_pad = jnp.concatenate([zero_rows, value_all], axis=0)
    seg_pad = jnp.concatenate([jnp.full((margin,), -1, jnp.int32), segments.astype(jnp.int32)], axis=0)
    span = margin + qblock

    def one_block(carry, block_index):
        key_acc, value_acc = carry
        first_row = (block_index * qblock).astype(jnp.int32)
        query_blk = lax.dynamic_slice_in_dim(query_all, first_row, qblock, 0)
        grad_blk = lax.dynamic_slice_in_dim(grad_all, first_row, qblock, 0)
        rows_blk = lax.dynamic_slice_in_dim(rowsum, first_row, qblock, 0)
        query_seg = lax.dynamic_slice_in_dim(segments.astype(jnp.int32), first_row, qblock, 0)
        key_blk = lax.dynamic_slice_in_dim(key_pad, first_row, span, 0)
        value_blk = lax.dynamic_slice_in_dim(value_pad, first_row, span, 0)
        key_seg = lax.dynamic_slice_in_dim(seg_pad, first_row, span, 0)
        query_pos = first_row + jnp.arange(qblock, dtype=jnp.int32)
        key_pos = first_row - margin + jnp.arange(span, dtype=jnp.int32)
        spacing = query_pos[:, None] - key_pos[None, :]
        allowed = (spacing >= 0) & (spacing < WINDOW) & (key_pos[None, :] >= 0) & (query_seg[:, None] == key_seg[None, :])
        raw_score = jnp.einsum('qhd,khd->hqk', query_blk, key_blk) * query_scale
        bent_score = jnp.tanh(raw_score / soft_cap)
        weight = jnp.where(allowed[None], jnp.exp(soft_cap * bent_score), jnp.zeros_like(bent_score))
        row_total = jnp.sum(weight, axis=2, keepdims=True)
        prob_full = weight / row_total
        prob_low = round_low(prob_full)
        value_grad = jnp.einsum('hqk,qhd->khd', prob_low, grad_blk)
        grad_prob = jnp.einsum('qhd,khd->hqk', grad_blk, value_blk)
        grad_score = round_low(prob_full * (grad_prob - rows_blk.T[:, :, None]) * (1.0 - bent_score * bent_score))
        query_grad = jnp.einsum('hqk,khd->qhd', grad_score, key_blk) * query_scale
        key_grad = jnp.einsum('hqk,qhd->khd', grad_score, query_blk) * query_scale
        key_old = lax.dynamic_slice_in_dim(key_acc, first_row, span, 0)
        value_old = lax.dynamic_slice_in_dim(value_acc, first_row, span, 0)
        key_acc = lax.dynamic_update_slice_in_dim(key_acc, key_old + key_grad, first_row, 0)
        value_acc = lax.dynamic_update_slice_in_dim(value_acc, value_old + value_grad, first_row, 0)
        return (key_acc, value_acc), query_grad.astype(jnp.bfloat16)

    start_acc = jnp.zeros((margin + length, HEADS, HEAD_DIM), jnp.float32)
    (key_acc, value_acc), query_parts = lax.scan(one_block, (start_acc, start_acc), jnp.arange(length // qblock, dtype=jnp.int32))
    grad_query = query_parts.reshape(length, HEADS * HEAD_DIM)
    head_key = round_low(key_acc[margin:])
    head_value = round_low(value_acc[margin:])
    grad_key = head_key.reshape(length, KV_HEADS, groups, HEAD_DIM).sum(axis=2).astype(jnp.bfloat16).reshape(length, KV_HEADS * HEAD_DIM)
    grad_value = head_value.reshape(length, KV_HEADS, groups, HEAD_DIM).sum(axis=2).astype(jnp.bfloat16).reshape(length, KV_HEADS * HEAD_DIM)
    return (grad_query, grad_key, grad_value)
```

```python
import functools

import jax
import jax.numpy as jnp
from jax import lax
from jax.experimental import pallas as pl
from jax.experimental.pallas import tpu as pltpu
from jax.sharding import PartitionSpec as P

HEAD_DIM = 256
WINDOW = 512
SCORE_SCALE = 0.0625
SOFT_CAP = 50.0
RING = 8
ROWS = 128
BACK = WINDOW // ROWS
SPAN = (BACK + 1) * ROWS
PAIR = 2 * HEAD_DIM
MESH = pl.DeviceIdType.MESH


def rows_of(index, count=1):
    return pl.ds(pl.multiple_of(index * ROWS, ROWS), count * ROWS)


def cols_of(index, width):
    return pl.ds(pl.multiple_of(index * width, width), width)


def kernel(
    halves,
    query_ref, key_ref, value_ref, grad_ref, dots_ref, seg_ref,
    gq_ref, gk_ref, gv_ref,
    q_buf, d_buf, k_buf, v_buf, kt_buf, r_src, r_buf, seg_buf, low_buf,
    k_acc, v_acc, gq_buf, gkv_buf, halo_out, halo_in,
    send_kv, send_qd, send_r, recv_kv, recv_qd, recv_r, seg_sem,
    halo_send, halo_recv, back_send, back_recv,
    out_send, out_recv,
):
    blk, uly = lax.axis_index("blk"), lax.axis_index("uly")
    side, z = uly // RING, lax.rem(uly, RING)
    half = blk * 2 + side
    has_prev, has_next = half > 0, half < halves - 1

    def device(h, zz):
        return (h // 2, lax.rem(h, 2) * RING + zz)

    def peer_of(offset):
        return lax.rem(z + offset, RING)

    prev_dev, next_dev = device(half - 1, z), device(half + 1, z)

    def key_copy(i):
        src, buf = ((key_ref, k_buf), (value_ref, v_buf))[i]
        return pltpu.make_async_copy(
            src.at[:, cols_of(z, HEAD_DIM)], buf.at[rows_of(BACK + z)], recv_kv.at[i, z]
        )

    def query_copy(i):
        src, buf = ((query_ref, q_buf), (grad_ref, d_buf))[i]
        return pltpu.make_async_copy(
            src.at[:, cols_of(z, PAIR)], buf.at[rows_of(z)], recv_qd.at[i, z]
        )

    for i in range(2):
        key_copy(i).start()
        query_copy(i).start()
    own_seg = pltpu.make_async_copy(seg_ref.at[half], seg_buf.at[1], seg_sem.at[1])
    own_seg.start()

    @pl.when(has_prev)
    def _():
        pltpu.make_async_copy(seg_ref.at[half - 1], seg_buf.at[0], seg_sem.at[0]).start()

    barrier = pltpu.get_barrier_semaphore()
    for offset in range(1, RING):
        pl.semaphore_signal(
            barrier, inc=1, device_id=device(half, peer_of(offset)), device_id_type=MESH
        )

    @pl.when(has_prev)
    def _():
        pl.semaphore_signal(barrier, inc=1, device_id=prev_dev, device_id_type=MESH)

    @pl.when(has_next)
    def _():
        pl.semaphore_signal(barrier, inc=1, device_id=next_dev, device_id_type=MESH)

    dots = dots_ref[...].astype(jnp.float32)
    turned = jnp.concatenate([dots, jnp.zeros((ROWS, ROWS - dots.shape[1]), jnp.float32)], axis=1).T
    for p in range(RING):
        r_src[p] = jnp.concatenate(
            [turned[2 * p : 2 * p + 2], jnp.zeros((6, ROWS), jnp.float32)], axis=0
        )
    r_buf[z] = r_src[z]

    pl.semaphore_wait(
        barrier, RING - 1 + has_prev.astype(jnp.int32) + has_next.astype(jnp.int32)
    )

    def send(src, dst, send_sem, recv_sem, dev):
        return pltpu.make_async_remote_copy(
            src_ref=src, dst_ref=dst, send_sem=send_sem, recv_sem=recv_sem,
            device_id=dev, device_id_type=MESH,
        )

    def send_keys(i, offset):
        src, buf = ((key_ref, k_buf), (value_ref, v_buf))[i]
        p = peer_of(offset)
        return send(
            src.at[:, cols_of(p, HEAD_DIM)], buf.at[rows_of(BACK + z)],
            send_kv.at[i, offset], recv_kv.at[i, z], device(half, p),
        )

    def send_queries(i, offset):
        src, buf = ((query_ref, q_buf), (grad_ref, d_buf))[i]
        p = peer_of(offset)
        return send(
            src.at[:, cols_of(p, PAIR)], buf.at[rows_of(z)],
            send_qd.at[i, offset], recv_qd.at[i, z], device(half, p),
        )

    def send_dots(offset):
        p = peer_of(offset)
        return send(
            r_src.at[p], r_buf.at[z], send_r.at[offset], recv_r.at[z], device(half, p)
        )

    order = (4, 3, 5, 2, 6, 1, 7)
    for offset in order:
        for i in range(2):
            send_keys(i, offset).start()
    for offset in order:
        send_dots(offset).start()
        for i in range(2):
            send_queries(i, offset).start()

    own_seg.wait()

    @pl.when(has_prev)
    def _():
        pltpu.make_async_copy(seg_ref.at[half], seg_buf.at[0], seg_sem.at[0]).wait()

    @pl.when(jnp.logical_not(has_prev))
    def _():
        seg_buf[0] = jnp.full((RING, ROWS), -1, jnp.int32)
        k_buf[: BACK * ROWS] = jnp.zeros((BACK * ROWS, HEAD_DIM), jnp.bfloat16)
        v_buf[: BACK * ROWS] = jnp.zeros((BACK * ROWS, HEAD_DIM), jnp.bfloat16)

    before, here = seg_buf[0], seg_buf[1]
    first = jnp.zeros((RING, ROWS), jnp.int32)
    for doc in range(16):
        below = jnp.sum(
            (before < doc).astype(jnp.int32) + (here < doc).astype(jnp.int32),
            keepdims=True,
        )
        first = jnp.where(here == doc, below, first)
    tile_of = lax.broadcasted_iota(jnp.int32, (RING, ROWS), 0)
    lane_of = lax.broadcasted_iota(jnp.int32, (RING, ROWS), 1)
    origin = (RING - BACK) * ROWS + tile_of * ROWS
    low = jnp.maximum(first - origin, lane_of + 1)
    for t in range(RING):
        low_buf[t] = jnp.broadcast_to(low[t : t + 1], (8, ROWS))

    k_acc[...] = jnp.zeros(k_acc.shape, jnp.float32)
    v_acc[...] = jnp.zeros(v_acc.shape, jnp.float32)

    def wait_keys(j):
        key_slot, value_slot = k_buf.at[rows_of(BACK + j)], v_buf.at[rows_of(BACK + j)]
        pltpu.make_async_copy(key_slot, key_slot, recv_kv.at[0, j]).wait()
        pltpu.make_async_copy(value_slot, value_slot, recv_kv.at[1, j]).wait()

    def turn_keys(index):
        kt_buf[:, rows_of(index)] = k_buf[rows_of(index)].T

    def send_halo(i, j):
        buf = (k_buf, v_buf)[i]
        return send(
            buf.at[rows_of(RING + j)], buf.at[rows_of(j)],
            halo_send.at[i, j], halo_recv.at[i, j], next_dev,
        )

    for j in range(BACK):
        wait_keys(RING - BACK + j)

        @pl.when(has_next)
        def _(j=j):
            send_halo(0, j).start()
            send_halo(1, j).start()

    def turn_late(j, carry):
        turn_keys(RING + j)
        return carry

    lax.fori_loop(0, BACK, turn_late, 0)

    def take_early(j, carry):
        wait_keys(j)
        turn_keys(BACK + j)
        return carry

    lax.fori_loop(0, RING - BACK, take_early, 0)

    @pl.when(has_prev)
    def _():
        for j in range(BACK):
            for i in range(2):
                slot = (k_buf, v_buf)[i].at[rows_of(j)]
                pltpu.make_async_copy(slot, slot, halo_recv.at[i, j]).wait()

    def turn_halo(j, carry):
        turn_keys(j)
        return carry

    lax.fori_loop(0, BACK, turn_halo, 0)

    def send_out(kind, j):
        buf, out, width = (
            (gq_buf.at[rows_of(j)], gq_ref, PAIR),
            (gkv_buf.at[0, rows_of(j)], gk_ref, HEAD_DIM),
            (gkv_buf.at[1, rows_of(j)], gv_ref, HEAD_DIM),
        )[kind]
        dst = out.at[:, cols_of(z, width)]
        remote = send(buf, dst, out_send.at[kind, j], out_recv.at[kind, z], device(half, j))
        local = pltpu.make_async_copy(buf, dst, out_recv.at[kind, z])
        return remote, local

    def start_out(kind, j):
        remote, local = send_out(kind, j)

        @pl.when(j != z)
        def _():
            remote.start()

        @pl.when(j == z)
        def _():
            local.start()

    def nt_dot(a, b):
        return lax.dot_general(
            a, b, (((1,), (1,)), ((), ())), preferred_element_type=jnp.float32
        )

    def dot(a, b):
        return jnp.dot(a, b, preferred_element_type=jnp.float32)

    def finish_keys(j, extra_key, extra_value):
        rows = rows_of(BACK + j)
        gkv_buf[0, rows_of(j)] = (
            (k_acc[rows] * SCORE_SCALE + extra_key).astype(jnp.bfloat16)
        )
        gkv_buf[1, rows_of(j)] = (v_acc[rows] + extra_value).astype(jnp.bfloat16)
        start_out(1, j)
        start_out(2, j)

    def tile(t, carry):
        for i in range(2):
            slot = (q_buf, d_buf)[i].at[rows_of(t)]
            pltpu.make_async_copy(slot, slot, recv_qd.at[i, t]).wait()

        @pl.when(t != z)
        def _():
            pltpu.make_async_copy(r_buf.at[t], r_buf.at[t], recv_r.at[t]).wait()

        span = rows_of(t, BACK + 1)
        queries, grads = q_buf[rows_of(t)], d_buf[rows_of(t)]
        queries = jnp.concatenate([queries[:, :HEAD_DIM], queries[:, HEAD_DIM:]], axis=0)
        grads = jnp.concatenate([grads[:, :HEAD_DIM], grads[:, HEAD_DIM:]], axis=0)
        sums = r_buf[t]
        sums = jnp.concatenate([sums[0:1], sums[1:2]], axis=1)
        least = low_buf[t][0:1]
        least = jnp.concatenate([least, least], axis=1)
        keys = k_buf[span]
        bent = jnp.tanh(nt_dot(keys, queries) * (SCORE_SCALE / SOFT_CAP))
        place = lax.broadcasted_iota(jnp.int32, (SPAN, 2 * ROWS), 0)
        column = lax.broadcasted_iota(jnp.int32, (SPAN, 2 * ROWS), 1)
        most = WINDOW + jnp.where(column < ROWS, column, column - ROWS)
        allowed = (place >= least) & (place <= most)
        weight = jnp.where(allowed, jnp.exp(SOFT_CAP * bent), 0.0)
        prob = weight * (1.0 / jnp.sum(weight, axis=0, keepdims=True))
        grad_prob = nt_dot(v_buf[span], grads)
        grad_score = (prob * (grad_prob - sums) * (1.0 - bent * bent)).astype(jnp.bfloat16)
        v_acc[span] += dot(prob.astype(jnp.bfloat16), grads)
        k_acc[span] += dot(grad_score, queries)
        turned_grad = dot(kt_buf[:, span], grad_score)
        query_grad = (turned_grad * SCORE_SCALE).T.astype(jnp.bfloat16)
        gq_buf[rows_of(t), :HEAD_DIM] = query_grad[:ROWS]
        gq_buf[rows_of(t), HEAD_DIM:] = query_grad[ROWS:]
        start_out(0, t)
        return carry

    def send_back(i):
        return send(
            halo_out.at[i], halo_in.at[i], back_send.at[i], back_recv.at[i], prev_dev
        )

    lax.fori_loop(0, BACK, tile, 0)

    @pl.when(has_prev)
    def _():
        halo_out[0] = (k_acc[: BACK * ROWS] * SCORE_SCALE).astype(jnp.bfloat16)
        halo_out[1] = v_acc[: BACK * ROWS].astype(jnp.bfloat16)
        send_back(0).start()
        send_back(1).start()

    def late_tile(t, carry):
        tile(t, carry)
        finish_keys(t - BACK, 0.0, 0.0)
        return carry

    lax.fori_loop(BACK, RING, late_tile, 0)

    @pl.when(has_next)
    def _():
        for i in range(2):
            pltpu.make_async_copy(halo_in.at[i], halo_in.at[i], back_recv.at[i]).wait()

    @pl.when(jnp.logical_not(has_next))
    def _():
        halo_in[...] = jnp.zeros(halo_in.shape, jnp.bfloat16)

    def last_keys(j, carry):
        rows = rows_of(j)
        finish_keys(
            RING - BACK + j,
            halo_in[0, rows].astype(jnp.float32),
            halo_in[1, rows].astype(jnp.float32),
        )
        return carry

    lax.fori_loop(0, BACK, last_keys, 0)

    for offset in order:
        for i in range(2):
            send_keys(i, offset).wait_send()
            send_queries(i, offset).wait_send()
        send_dots(offset).wait_send()

    @pl.when(has_next)
    def _():
        for j in range(BACK):
            for i in range(2):
                send_halo(i, j).wait_send()

    @pl.when(has_prev)
    def _():
        for i in range(2):
            send_back(i).wait_send()

    def drain(j, carry):
        for kind in range(3):
            remote, _ = send_out(kind, j)

            @pl.when(j != z)
            def _(remote=remote):
                remote.wait_send()

            out, width = ((gq_ref, PAIR), (gk_ref, HEAD_DIM), (gv_ref, HEAD_DIM))[kind]
            landed = out.at[:, cols_of(j, width)]
            pltpu.make_async_copy(landed, landed, out_recv.at[kind, j]).wait()
        return carry

    lax.fori_loop(0, RING, drain, 0)


def per_device(halves, query_in, key_in, value_in, grad_out, row_dot, segments):
    here = pl.BlockSpec(memory_space=pl.ANY)
    low, wide = jnp.bfloat16, jnp.float32
    outs = tuple(jax.ShapeDtypeStruct(a.shape, low) for a in (query_in, key_in, value_in))
    blocks = segments.reshape(halves, RING, ROWS)
    sem = pltpu.SemaphoreType.DMA
    tokens, reach = RING * ROWS, (RING + BACK) * ROWS
    flops = 5 * 2 * RING * SPAN * 2 * ROWS * HEAD_DIM
    return pl.pallas_call(
        functools.partial(kernel, halves),
        out_shape=outs,
        in_specs=[here] * 4 + [pl.BlockSpec(memory_space=pltpu.VMEM), here],
        out_specs=(here,) * 3,
        scratch_shapes=[
            pltpu.VMEM((tokens, PAIR), low),
            pltpu.VMEM((tokens, PAIR), low),
            pltpu.VMEM((reach, HEAD_DIM), low),
            pltpu.VMEM((reach, HEAD_DIM), low),
            pltpu.VMEM((HEAD_DIM, reach), low),
            pltpu.VMEM((RING, 8, ROWS), wide),
            pltpu.VMEM((RING, 8, ROWS), wide),
            pltpu.VMEM((2, RING, ROWS), jnp.int32),
            pltpu.VMEM((RING, 8, ROWS), jnp.int32),
            pltpu.VMEM((reach, HEAD_DIM), wide),
            pltpu.VMEM((reach, HEAD_DIM), wide),
            pltpu.VMEM((tokens, PAIR), low),
            pltpu.VMEM((2, tokens, HEAD_DIM), low),
            pltpu.VMEM((2, BACK * ROWS, HEAD_DIM), low),
            pltpu.VMEM((2, BACK * ROWS, HEAD_DIM), low),
            sem((2, RING)), sem((2, RING)), sem((RING,)),
            sem((2, RING)), sem((2, RING)), sem((RING,)), sem((2,)),
            sem((2, BACK)), sem((2, BACK)), sem((2,)), sem((2,)),
            sem((3, RING)), sem((3, RING)),
        ],
        compiler_params=pltpu.CompilerParams(
            collective_id=0, has_side_effects=True, vmem_limit_bytes=48 * 1024 * 1024
        ),
        cost_estimate=pl.CostEstimate(
            flops=flops, bytes_accessed=5 << 20, transcendentals=2 * RING * SPAN * 2 * ROWS
        ),
        name="window_backward",
    )(query_in, key_in, value_in, grad_out, row_dot, blocks)


def solution(mesh):
    rows = P(("blk", "uly"), None)
    halves = mesh.shape["blk"] * mesh.shape["uly"] // RING
    return jax.shard_map(
        functools.partial(per_device, halves),
        mesh=mesh,
        in_specs=(rows,) * 5 + (P(),),
        out_specs=(rows,) * 3,
        check_vma=False,
    )
```

```python
import functools

import jax
import jax.numpy as jnp
from jax import lax
from jax.experimental import pallas as pl
from jax.experimental.pallas import tpu as pltpu
from jax.sharding import PartitionSpec as P

HEAD_DIM = 256
WINDOW = 512
SCORE_SCALE = 0.0625
SOFT_CAP = 50.0
RING = 8
ROWS = 128
BACK = WINDOW // ROWS
SPAN = (BACK + 1) * ROWS
PAIR = 2 * HEAD_DIM
MESH = pl.DeviceIdType.MESH


def rows_of(index, count=1):
    return pl.ds(pl.multiple_of(index * ROWS, ROWS), count * ROWS)


def cols_of(index, width):
    return pl.ds(pl.multiple_of(index * width, width), width)


def kernel(
    halves,
    query_ref, key_ref, value_ref, grad_ref, dots_ref, seg_ref,
    gq_ref, gk_ref, gv_ref,
    q_buf, d_buf, k_buf, v_buf, kt_buf, dots_buf, r_src, r_buf, seg_buf, low_buf,
    k_acc, v_acc, gq_buf, gkv_buf, halo_out, halo_in,
    send_kv, send_qd, send_r, recv_kv, recv_qd, recv_r, seg_sem,
    halo_send, halo_recv, back_send, back_recv,
    out_send, out_recv,
):
    blk, uly = lax.axis_index("blk"), lax.axis_index("uly")
    side, z = uly // RING, lax.rem(uly, RING)
    half = blk * 2 + side
    has_prev, has_next = half > 0, half < halves - 1

    def device(h, zz):
        return (h // 2, lax.rem(h, 2) * RING + zz)

    def peer_of(offset):
        return lax.rem(z + offset, RING)

    prev_dev, next_dev = device(half - 1, z), device(half + 1, z)

    def key_copy(i):
        src, buf = ((key_ref, k_buf), (value_ref, v_buf))[i]
        return pltpu.make_async_copy(
            src.at[:, cols_of(z, HEAD_DIM)], buf.at[rows_of(BACK + z)], recv_kv.at[i, z]
        )

    def query_copy(i):
        src, buf = ((query_ref, q_buf), (grad_ref, d_buf))[i]
        return pltpu.make_async_copy(
            src.at[:, cols_of(z, PAIR)], buf.at[rows_of(z)], recv_qd.at[i, z]
        )

    for i in range(2):
        key_copy(i).start()
        query_copy(i).start()
    own_seg = pltpu.make_async_copy(seg_ref.at[half], seg_buf.at[1], seg_sem.at[1])
    own_seg.start()
    dots_copy = pltpu.make_async_copy(dots_ref, dots_buf, seg_sem.at[2])
    dots_copy.start()

    @pl.when(has_prev)
    def _():
        pltpu.make_async_copy(seg_ref.at[half - 1], seg_buf.at[0], seg_sem.at[0]).start()

    barrier = pltpu.get_barrier_semaphore()
    for offset in range(1, RING):
        pl.semaphore_signal(
            barrier, inc=1, device_id=device(half, peer_of(offset)), device_id_type=MESH
        )

    @pl.when(has_prev)
    def _():
        pl.semaphore_signal(barrier, inc=1, device_id=prev_dev, device_id_type=MESH)

    @pl.when(has_next)
    def _():
        pl.semaphore_signal(barrier, inc=1, device_id=next_dev, device_id_type=MESH)

    dots_copy.wait()
    turned = dots_buf[...].astype(jnp.float32)
    for p in range(RING):
        r_src[p] = jnp.concatenate(
            [turned[2 * p : 2 * p + 2], jnp.zeros((6, ROWS), jnp.float32)], axis=0
        )
    r_buf[z] = r_src[z]

    pl.semaphore_wait(
        barrier, RING - 1 + has_prev.astype(jnp.int32) + has_next.astype(jnp.int32)
    )

    def send(src, dst, send_sem, recv_sem, dev):
        return pltpu.make_async_remote_copy(
            src_ref=src, dst_ref=dst, send_sem=send_sem, recv_sem=recv_sem,
            device_id=dev, device_id_type=MESH,
        )

    def send_keys(i, offset):
        src, buf = ((key_ref, k_buf), (value_ref, v_buf))[i]
        p = peer_of(offset)
        return send(
            src.at[:, cols_of(p, HEAD_DIM)], buf.at[rows_of(BACK + z)],
            send_kv.at[i, offset], recv_kv.at[i, z], device(half, p),
        )

    def send_queries(i, offset):
        src, buf = ((query_ref, q_buf), (grad_ref, d_buf))[i]
        p = peer_of(offset)
        return send(
            src.at[:, cols_of(p, PAIR)], buf.at[rows_of(z)],
            send_qd.at[i, offset], recv_qd.at[i, z], device(half, p),
        )

    def send_dots(offset):
        p = peer_of(offset)
        return send(
            r_src.at[p], r_buf.at[z], send_r.at[offset], recv_r.at[z], device(half, p)
        )

    order = (4, 3, 5, 2, 6, 1, 7)
    for offset in order:
        for i in range(2):
            send_keys(i, offset).start()
    for offset in order:
        send_dots(offset).start()
        for i in range(2):
            send_queries(i, offset).start()

    own_seg.wait()

    @pl.when(has_prev)
    def _():
        pltpu.make_async_copy(seg_ref.at[half], seg_buf.at[0], seg_sem.at[0]).wait()

    @pl.when(jnp.logical_not(has_prev))
    def _():
        seg_buf[0] = jnp.full((RING, ROWS), -1, jnp.int32)
        k_buf[: BACK * ROWS] = jnp.zeros((BACK * ROWS, HEAD_DIM), jnp.bfloat16)
        v_buf[: BACK * ROWS] = jnp.zeros((BACK * ROWS, HEAD_DIM), jnp.bfloat16)

    before, here = seg_buf[0], seg_buf[1]
    first = jnp.zeros((RING, ROWS), jnp.int32)
    for doc in range(16):
        below = jnp.sum(
            (before < doc).astype(jnp.int32) + (here < doc).astype(jnp.int32),
            keepdims=True,
        )
        first = jnp.where(here == doc, below, first)
    tile_of = lax.broadcasted_iota(jnp.int32, (RING, ROWS), 0)
    lane_of = lax.broadcasted_iota(jnp.int32, (RING, ROWS), 1)
    origin = (RING - BACK) * ROWS + tile_of * ROWS
    low = jnp.maximum(first - origin, lane_of + 1)
    for t in range(RING):
        low_buf[t] = jnp.broadcast_to(low[t : t + 1], (8, ROWS))

    k_acc[...] = jnp.zeros(k_acc.shape, jnp.float32)
    v_acc[...] = jnp.zeros(v_acc.shape, jnp.float32)

    def wait_keys(j):
        key_slot, value_slot = k_buf.at[rows_of(BACK + j)], v_buf.at[rows_of(BACK + j)]
        pltpu.make_async_copy(key_slot, key_slot, recv_kv.at[0, j]).wait()
        pltpu.make_async_copy(value_slot, value_slot, recv_kv.at[1, j]).wait()

    def turn_keys(index):
        kt_buf[:, rows_of(index)] = k_buf[rows_of(index)].T

    def send_halo(i, j):
        buf = (k_buf, v_buf)[i]
        return send(
            buf.at[rows_of(RING + j)], buf.at[rows_of(j)],
            halo_send.at[i, j], halo_recv.at[i, j], next_dev,
        )

    for j in range(BACK):
        wait_keys(RING - BACK + j)

        @pl.when(has_next)
        def _(j=j):
            send_halo(0, j).start()
            send_halo(1, j).start()

    def turn_late(j, carry):
        turn_keys(RING + j)
        return carry

    lax.fori_loop(0, BACK, turn_late, 0)

    def take_early(j, carry):
        wait_keys(j)
        turn_keys(BACK + j)
        return carry

    lax.fori_loop(0, RING - BACK, take_early, 0)

    @pl.when(has_prev)
    def _():
        for j in range(BACK):
            for i in range(2):
                slot = (k_buf, v_buf)[i].at[rows_of(j)]
                pltpu.make_async_copy(slot, slot, halo_recv.at[i, j]).wait()

    def turn_halo(j, carry):
        turn_keys(j)
        return carry

    lax.fori_loop(0, BACK, turn_halo, 0)

    def send_out(kind, j):
        buf, out, width = (
            (gq_buf.at[rows_of(j)], gq_ref, PAIR),
            (gkv_buf.at[0, rows_of(j)], gk_ref, HEAD_DIM),
            (gkv_buf.at[1, rows_of(j)], gv_ref, HEAD_DIM),
        )[kind]
        dst = out.at[:, cols_of(z, width)]
        remote = send(buf, dst, out_send.at[kind, j], out_recv.at[kind, z], device(half, j))
        local = pltpu.make_async_copy(buf, dst, out_recv.at[kind, z])
        return remote, local

    def start_out(kind, j):
        remote, local = send_out(kind, j)

        @pl.when(j != z)
        def _():
            remote.start()

        @pl.when(j == z)
        def _():
            local.start()

    def nt_dot(a, b):
        return lax.dot_general(
            a, b, (((1,), (1,)), ((), ())), preferred_element_type=jnp.float32
        )

    def dot(a, b):
        return jnp.dot(a, b, preferred_element_type=jnp.float32)

    def finish_keys(j, extra_key, extra_value):
        rows = rows_of(BACK + j)
        gkv_buf[0, rows_of(j)] = (
            (k_acc[rows] * SCORE_SCALE + extra_key).astype(jnp.bfloat16)
        )
        gkv_buf[1, rows_of(j)] = (v_acc[rows] + extra_value).astype(jnp.bfloat16)
        start_out(1, j)
        start_out(2, j)

    def tile(t, carry):
        for i in range(2):
            slot = (q_buf, d_buf)[i].at[rows_of(t)]
            pltpu.make_async_copy(slot, slot, recv_qd.at[i, t]).wait()

        @pl.when(t != z)
        def _():
            pltpu.make_async_copy(r_buf.at[t], r_buf.at[t], recv_r.at[t]).wait()

        span = rows_of(t, BACK + 1)
        queries, grads = q_buf[rows_of(t)], d_buf[rows_of(t)]
        queries = jnp.concatenate([queries[:, :HEAD_DIM], queries[:, HEAD_DIM:]], axis=0)
        grads = jnp.concatenate([grads[:, :HEAD_DIM], grads[:, HEAD_DIM:]], axis=0)
        sums = r_buf[t]
        sums = jnp.concatenate([sums[0:1], sums[1:2]], axis=1)
        least = low_buf[t][0:1]
        least = jnp.concatenate([least, least], axis=1)
        keys = k_buf[span]
        bent = jnp.tanh(nt_dot(keys, queries) * (SCORE_SCALE / SOFT_CAP))
        place = lax.broadcasted_iota(jnp.int32, (SPAN, 2 * ROWS), 0)
        column = lax.broadcasted_iota(jnp.int32, (SPAN, 2 * ROWS), 1)
        most = WINDOW + jnp.where(column < ROWS, column, column - ROWS)
        allowed = (place >= least) & (place <= most)
        weight = jnp.where(allowed, jnp.exp(SOFT_CAP * bent), 0.0)
        prob = weight * (1.0 / jnp.sum(weight, axis=0, keepdims=True))
        grad_prob = nt_dot(v_buf[span], grads)
        grad_score = (prob * (grad_prob - sums) * (1.0 - bent * bent)).astype(jnp.bfloat16)
        v_acc[span] += dot(prob.astype(jnp.bfloat16), grads)
        k_acc[span] += dot(grad_score, queries)
        turned_grad = dot(kt_buf[:, span], grad_score)
        query_grad = (turned_grad * SCORE_SCALE).T.astype(jnp.bfloat16)
        gq_buf[rows_of(t), :HEAD_DIM] = query_grad[:ROWS]
        gq_buf[rows_of(t), HEAD_DIM:] = query_grad[ROWS:]
        start_out(0, t)
        return carry

    def send_back(i, j):
        return send(
            halo_out.at[i, rows_of(j)], halo_in.at[i, rows_of(j)],
            back_send.at[i, j], back_recv.at[i, j], prev_dev,
        )

    def early_tile(t, carry):
        tile(t, carry)

        @pl.when(has_prev)
        def _():
            rows = rows_of(t)
            halo_out[0, rows] = (k_acc[rows] * SCORE_SCALE).astype(jnp.bfloat16)
            halo_out[1, rows] = v_acc[rows].astype(jnp.bfloat16)
            send_back(0, t).start()
            send_back(1, t).start()

        return carry

    lax.fori_loop(0, BACK, early_tile, 0)

    def late_tile(t, carry):
        tile(t, carry)
        finish_keys(t - BACK, 0.0, 0.0)
        return carry

    lax.fori_loop(BACK, RING, late_tile, 0)

    @pl.when(jnp.logical_not(has_next))
    def _():
        halo_in[...] = jnp.zeros(halo_in.shape, jnp.bfloat16)

    def last_keys(j, carry):
        rows = rows_of(j)

        @pl.when(has_next)
        def _():
            for i in range(2):
                slot = halo_in.at[i, rows]
                pltpu.make_async_copy(slot, slot, back_recv.at[i, j]).wait()

        finish_keys(
            RING - BACK + j,
            halo_in[0, rows].astype(jnp.float32),
            halo_in[1, rows].astype(jnp.float32),
        )
        return carry

    lax.fori_loop(0, BACK, last_keys, 0)

    for offset in order:
        for i in range(2):
            send_keys(i, offset).wait_send()
            send_queries(i, offset).wait_send()
        send_dots(offset).wait_send()

    @pl.when(has_next)
    def _():
        for j in range(BACK):
            for i in range(2):
                send_halo(i, j).wait_send()

    @pl.when(has_prev)
    def _():
        for j in range(BACK):
            for i in range(2):
                send_back(i, j).wait_send()

    def drain(j, carry):
        for kind in range(3):
            remote, _ = send_out(kind, j)

            @pl.when(j != z)
            def _(remote=remote):
                remote.wait_send()

            out, width = ((gq_ref, PAIR), (gk_ref, HEAD_DIM), (gv_ref, HEAD_DIM))[kind]
            landed = out.at[:, cols_of(j, width)]
            pltpu.make_async_copy(landed, landed, out_recv.at[kind, j]).wait()
        return carry

    lax.fori_loop(0, RING, drain, 0)


def place(*refs):
    ins, outs, bufs, get, put = refs[:3], refs[3:6], refs[6:9], refs[9], refs[10]
    parts = [(i, j) for j in range(4) for i in range(3)]

    def step(i, j, out):
        rows = pl.ds(j * (ROWS // 4), ROWS // 4)
        src, dst, sems = (bufs[i], outs[i], put) if out else (ins[i], bufs[i], get)
        return pltpu.make_async_copy(src.at[rows], dst.at[rows], sems.at[i, j])

    for i, j in parts:
        step(i, j, False).start()
    for i, j in parts:
        step(i, j, False).wait()
        step(i, j, True).start()
    for i, j in parts:
        step(i, j, True).wait()


def per_device(halves, query_in, key_in, value_in, grad_out, row_dot, segments):
    here = pl.BlockSpec(memory_space=pl.ANY)
    low, wide = jnp.bfloat16, jnp.float32
    outs = tuple(jax.ShapeDtypeStruct(a.shape, low) for a in (query_in, key_in, value_in))
    blocks = segments.reshape(halves, RING, ROWS)
    sem = pltpu.SemaphoreType.DMA
    tokens, reach = RING * ROWS, (RING + BACK) * ROWS
    flops = 5 * 2 * RING * SPAN * 2 * ROWS * HEAD_DIM
    grads = pl.pallas_call(
        functools.partial(kernel, halves),
        out_shape=outs,
        in_specs=[here] * 6,
        out_specs=(here,) * 3,
        scratch_shapes=[
            pltpu.VMEM((tokens, PAIR), low),
            pltpu.VMEM((tokens, PAIR), low),
            pltpu.VMEM((reach, HEAD_DIM), low),
            pltpu.VMEM((reach, HEAD_DIM), low),
            pltpu.VMEM((HEAD_DIM, reach), low),
            pltpu.VMEM((2 * RING, ROWS), low),
            pltpu.VMEM((RING, 8, ROWS), wide),
            pltpu.VMEM((RING, 8, ROWS), wide),
            pltpu.VMEM((2, RING, ROWS), jnp.int32),
            pltpu.VMEM((RING, 8, ROWS), jnp.int32),
            pltpu.VMEM((reach, HEAD_DIM), wide),
            pltpu.VMEM((reach, HEAD_DIM), wide),
            pltpu.VMEM((tokens, PAIR), low),
            pltpu.VMEM((2, tokens, HEAD_DIM), low),
            pltpu.VMEM((2, BACK * ROWS, HEAD_DIM), low),
            pltpu.VMEM((2, BACK * ROWS, HEAD_DIM), low),
            sem((2, RING)), sem((2, RING)), sem((RING,)),
            sem((2, RING)), sem((2, RING)), sem((RING,)), sem((3,)),
            sem((2, BACK)), sem((2, BACK)), sem((2, BACK)), sem((2, BACK)),
            sem((3, RING)), sem((3, RING)),
        ],
        compiler_params=pltpu.CompilerParams(
            collective_id=0, has_side_effects=True, vmem_limit_bytes=62 * 1024 * 1024
        ),
        cost_estimate=pl.CostEstimate(
            flops=flops, bytes_accessed=5 << 20, transcendentals=2 * RING * SPAN * 2 * ROWS
        ),
        name="window_backward",
    )(query_in, key_in, value_in, grad_out, row_dot.T, blocks)
    return pl.pallas_call(
        place,
        out_shape=outs,
        in_specs=[here] * 3,
        out_specs=(here,) * 3,
        scratch_shapes=[pltpu.VMEM(o.shape, low) for o in outs] + [sem((3, 4))] * 2,
        name="place",
    )(*grads)


def solution(mesh):
    rows = P(("blk", "uly"), None)
    halves = mesh.shape["blk"] * mesh.shape["uly"] // RING
    return jax.shard_map(
        functools.partial(per_device, halves),
        mesh=mesh,
        in_specs=(rows,) * 5 + (P(),),
        out_specs=(rows,) * 3,
        check_vma=False,
    )
```

```python
import functools

import jax
import jax.numpy as jnp
from jax import lax
from jax.experimental import pallas as pl
from jax.experimental.pallas import tpu as pltpu
from jax.sharding import PartitionSpec as P

HEAD_DIM = 256
WINDOW = 512
SCORE_SCALE = 0.0625
SOFT_CAP = 50.0
RING = 8
ROWS = 128
BACK = WINDOW // ROWS
SPAN = (BACK + 1) * ROWS
PAIR = 2 * HEAD_DIM
MESH = pl.DeviceIdType.MESH


def rows_of(index, count=1):
    return pl.ds(pl.multiple_of(index * ROWS, ROWS), count * ROWS)


def cols_of(index, width):
    return pl.ds(pl.multiple_of(index * width, width), width)


def kernel(
    halves,
    query_ref, key_ref, value_ref, grad_ref, dots_ref, seg_ref,
    gq_ref, gk_ref, gv_ref,
    q_buf, d_buf, k_buf, v_buf, kt_buf, dots_buf, r_src, r_buf, seg_buf, low_buf,
    k_acc, v_acc, gq_buf, gkv_buf, halo_out, halo_in,
    send_kv, send_qd, send_r, recv_kv, recv_qd, recv_r, seg_sem,
    halo_send, halo_recv, back_send, back_recv,
    out_send, out_recv,
):
    blk, uly = lax.axis_index("blk"), lax.axis_index("uly")
    side, z = uly // RING, lax.rem(uly, RING)
    half = blk * 2 + side
    has_prev, has_next = half > 0, half < halves - 1

    def device(h, zz):
        return (h // 2, lax.rem(h, 2) * RING + zz)

    def peer_of(offset):
        return lax.rem(z + offset, RING)

    prev_dev, next_dev = device(half - 1, z), device(half + 1, z)

    barrier = pltpu.get_barrier_semaphore()
    for offset in range(1, RING):
        pl.semaphore_signal(
            barrier, inc=1, device_id=device(half, peer_of(offset)), device_id_type=MESH
        )

    @pl.when(has_prev)
    def _():
        pl.semaphore_signal(barrier, inc=1, device_id=prev_dev, device_id_type=MESH)

    @pl.when(has_next)
    def _():
        pl.semaphore_signal(barrier, inc=1, device_id=next_dev, device_id_type=MESH)

    def key_copy(i):
        src, buf = ((key_ref, k_buf), (value_ref, v_buf))[i]
        return pltpu.make_async_copy(
            src.at[:, cols_of(z, HEAD_DIM)], buf.at[rows_of(BACK + z)], recv_kv.at[i, z]
        )

    def query_copy(i):
        src, buf = ((query_ref, q_buf), (grad_ref, d_buf))[i]
        return pltpu.make_async_copy(
            src.at[:, cols_of(z, PAIR)], buf.at[rows_of(z)], recv_qd.at[i, z]
        )

    for i in range(2):
        key_copy(i).start()
        query_copy(i).start()
    own_seg = pltpu.make_async_copy(seg_ref.at[half], seg_buf.at[1], seg_sem.at[1])
    own_seg.start()
    dots_copy = pltpu.make_async_copy(dots_ref, dots_buf, seg_sem.at[2])
    dots_copy.start()

    @pl.when(has_prev)
    def _():
        pltpu.make_async_copy(seg_ref.at[half - 1], seg_buf.at[0], seg_sem.at[0]).start()

    dots_copy.wait()
    turned = dots_buf[...].astype(jnp.float32)
    for p in range(RING):
        r_src[p] = jnp.concatenate(
            [turned[2 * p : 2 * p + 2], jnp.zeros((6, ROWS), jnp.float32)], axis=0
        )
    r_buf[z] = r_src[z]

    pl.semaphore_wait(
        barrier, RING - 1 + has_prev.astype(jnp.int32) + has_next.astype(jnp.int32)
    )

    def send(src, dst, send_sem, recv_sem, dev):
        return pltpu.make_async_remote_copy(
            src_ref=src, dst_ref=dst, send_sem=send_sem, recv_sem=recv_sem,
            device_id=dev, device_id_type=MESH,
        )

    def send_keys(i, offset):
        src, buf = ((key_ref, k_buf), (value_ref, v_buf))[i]
        p = peer_of(offset)
        return send(
            src.at[:, cols_of(p, HEAD_DIM)], buf.at[rows_of(BACK + z)],
            send_kv.at[i, offset], recv_kv.at[i, z], device(half, p),
        )

    def send_queries(i, offset):
        src, buf = ((query_ref, q_buf), (grad_ref, d_buf))[i]
        p = peer_of(offset)
        return send(
            src.at[:, cols_of(p, PAIR)], buf.at[rows_of(z)],
            send_qd.at[i, offset], recv_qd.at[i, z], device(half, p),
        )

    def send_dots(offset):
        p = peer_of(offset)
        return send(
            r_src.at[p], r_buf.at[z], send_r.at[offset], recv_r.at[z], device(half, p)
        )

    order = (1, 7, 2, 6, 3, 5, 4)
    for offset in order:
        for i in range(2):
            send_keys(i, offset).start()
    for offset in order:
        send_dots(offset).start()
        for i in range(2):
            send_queries(i, offset).start()

    own_seg.wait()

    @pl.when(has_prev)
    def _():
        pltpu.make_async_copy(seg_ref.at[half], seg_buf.at[0], seg_sem.at[0]).wait()

    @pl.when(jnp.logical_not(has_prev))
    def _():
        seg_buf[0] = jnp.full((RING, ROWS), -1, jnp.int32)
        k_buf[: BACK * ROWS] = jnp.zeros((BACK * ROWS, HEAD_DIM), jnp.bfloat16)
        v_buf[: BACK * ROWS] = jnp.zeros((BACK * ROWS, HEAD_DIM), jnp.bfloat16)

    before, here = seg_buf[0], seg_buf[1]
    first = jnp.zeros((RING, ROWS), jnp.int32)
    for doc in range(16):
        below = jnp.sum(
            (before < doc).astype(jnp.int32) + (here < doc).astype(jnp.int32),
            keepdims=True,
        )
        first = jnp.where(here == doc, below, first)
    tile_of = lax.broadcasted_iota(jnp.int32, (RING, ROWS), 0)
    lane_of = lax.broadcasted_iota(jnp.int32, (RING, ROWS), 1)
    origin = (RING - BACK) * ROWS + tile_of * ROWS
    low = jnp.maximum(first - origin, lane_of + 1)
    for t in range(RING):
        low_buf[t] = jnp.broadcast_to(low[t : t + 1], (8, ROWS))

    k_acc[...] = jnp.zeros(k_acc.shape, jnp.float32)
    v_acc[...] = jnp.zeros(v_acc.shape, jnp.float32)

    def wait_keys(j):
        key_slot, value_slot = k_buf.at[rows_of(BACK + j)], v_buf.at[rows_of(BACK + j)]
        pltpu.make_async_copy(key_slot, key_slot, recv_kv.at[0, j]).wait()
        pltpu.make_async_copy(value_slot, value_slot, recv_kv.at[1, j]).wait()

    def turn_keys(index):
        kt_buf[:, rows_of(index)] = k_buf[rows_of(index)].T

    def send_halo(i, j):
        buf = (k_buf, v_buf)[i]
        return send(
            buf.at[rows_of(RING + j)], buf.at[rows_of(j)],
            halo_send.at[i, j], halo_recv.at[i, j], next_dev,
        )

    for j in range(BACK):
        wait_keys(RING - BACK + j)

        @pl.when(has_next)
        def _(j=j):
            send_halo(0, j).start()
            send_halo(1, j).start()

    def turn_late(j, carry):
        turn_keys(RING + j)
        return carry

    lax.fori_loop(0, BACK, turn_late, 0)

    def take_early(j, carry):
        wait_keys(j)
        turn_keys(BACK + j)
        return carry

    lax.fori_loop(0, RING - BACK, take_early, 0)

    @pl.when(has_prev)
    def _():
        for j in range(BACK):
            for i in range(2):
                slot = (k_buf, v_buf)[i].at[rows_of(j)]
                pltpu.make_async_copy(slot, slot, halo_recv.at[i, j]).wait()

    def turn_halo(j, carry):
        turn_keys(j)
        return carry

    lax.fori_loop(0, BACK, turn_halo, 0)

    def send_out(kind, j):
        buf, out, width = (
            (gq_buf.at[rows_of(j)], gq_ref, PAIR),
            (gkv_buf.at[0, rows_of(j)], gk_ref, HEAD_DIM),
            (gkv_buf.at[1, rows_of(j)], gv_ref, HEAD_DIM),
        )[kind]
        dst = out.at[:, cols_of(z, width)]
        remote = send(buf, dst, out_send.at[kind, j], out_recv.at[kind, z], device(half, j))
        local = pltpu.make_async_copy(buf, dst, out_recv.at[kind, z])
        return remote, local

    def start_out(kind, j):
        remote, local = send_out(kind, j)

        @pl.when(j != z)
        def _():
            remote.start()

        @pl.when(j == z)
        def _():
            local.start()

    def nt_dot(a, b):
        return lax.dot_general(
            a, b, (((1,), (1,)), ((), ())), preferred_element_type=jnp.float32
        )

    def dot(a, b):
        return jnp.dot(a, b, preferred_element_type=jnp.float32)

    def finish_keys(j, extra_key, extra_value):
        rows = rows_of(BACK + j)
        gkv_buf[0, rows_of(j)] = (
            (k_acc[rows] * SCORE_SCALE + extra_key).astype(jnp.bfloat16)
        )
        gkv_buf[1, rows_of(j)] = (v_acc[rows] + extra_value).astype(jnp.bfloat16)
        start_out(1, j)
        start_out(2, j)

    def tile(t, carry):
        for i in range(2):
            slot = (q_buf, d_buf)[i].at[rows_of(t)]
            pltpu.make_async_copy(slot, slot, recv_qd.at[i, t]).wait()

        @pl.when(t != z)
        def _():
            pltpu.make_async_copy(r_buf.at[t], r_buf.at[t], recv_r.at[t]).wait()

        span = rows_of(t, BACK + 1)
        queries, grads = q_buf[rows_of(t)], d_buf[rows_of(t)]
        queries = jnp.concatenate([queries[:, :HEAD_DIM], queries[:, HEAD_DIM:]], axis=0)
        grads = jnp.concatenate([grads[:, :HEAD_DIM], grads[:, HEAD_DIM:]], axis=0)
        sums = r_buf[t]
        sums = jnp.concatenate([sums[0:1], sums[1:2]], axis=1)
        least = low_buf[t][0:1]
        least = jnp.concatenate([least, least], axis=1)
        keys = k_buf[span]
        bent = jnp.tanh(nt_dot(keys, queries) * (SCORE_SCALE / SOFT_CAP))
        place = lax.broadcasted_iota(jnp.int32, (SPAN, 2 * ROWS), 0)
        column = lax.broadcasted_iota(jnp.int32, (SPAN, 2 * ROWS), 1)
        most = WINDOW + jnp.where(column < ROWS, column, column - ROWS)
        allowed = (place >= least) & (place <= most)
        weight = jnp.where(allowed, jnp.exp(SOFT_CAP * bent), 0.0)
        prob = weight * (1.0 / jnp.sum(weight, axis=0, keepdims=True))
        grad_prob = nt_dot(v_buf[span], grads)
        grad_score = (prob * (grad_prob - sums) * (1.0 - bent * bent)).astype(jnp.bfloat16)
        v_acc[span] += dot(prob.astype(jnp.bfloat16), grads)
        k_acc[span] += dot(grad_score, queries)
        turned_grad = dot(kt_buf[:, span], grad_score)
        query_grad = (turned_grad * SCORE_SCALE).T.astype(jnp.bfloat16)
        gq_buf[rows_of(t), :HEAD_DIM] = query_grad[:ROWS]
        gq_buf[rows_of(t), HEAD_DIM:] = query_grad[ROWS:]
        start_out(0, t)
        return carry

    def send_back(i, j):
        return send(
            halo_out.at[i, rows_of(j)], halo_in.at[i, rows_of(j)],
            back_send.at[i, j], back_recv.at[i, j], prev_dev,
        )

    def step_of(t):
        ahead = lax.rem(t - z + RING, RING)
        return jnp.where(ahead * 2 <= RING, jnp.maximum(2 * ahead - 1, 0), 2 * (RING - ahead))

    def done_at(first, last):
        at = step_of(first)
        for t in range(first + 1, last + 1):
            at = jnp.maximum(at, step_of(t))
        return at

    halo_done = [done_at(0, j) for j in range(BACK)]
    own_done = [done_at(j, j + BACK) for j in range(RING - BACK)]

    def one_step(step, carry):
        near = (step + 1) // 2
        t = lax.rem(z + jnp.where(lax.rem(step, 2) == 1, near, RING - near), RING)
        tile(t, carry)
        for j in range(BACK):

            @pl.when((halo_done[j] == step) & has_prev)
            def _(j=j):
                rows = rows_of(j)
                halo_out[0, rows] = (k_acc[rows] * SCORE_SCALE).astype(jnp.bfloat16)
                halo_out[1, rows] = v_acc[rows].astype(jnp.bfloat16)
                send_back(0, j).start()
                send_back(1, j).start()

        for j in range(RING - BACK):

            @pl.when(own_done[j] == step)
            def _(j=j):
                finish_keys(j, 0.0, 0.0)

        return carry

    lax.fori_loop(0, RING, one_step, 0)

    @pl.when(jnp.logical_not(has_next))
    def _():
        halo_in[...] = jnp.zeros(halo_in.shape, jnp.bfloat16)

    def last_keys(j, carry):
        rows = rows_of(j)

        @pl.when(has_next)
        def _():
            for i in range(2):
                slot = halo_in.at[i, rows]
                pltpu.make_async_copy(slot, slot, back_recv.at[i, j]).wait()

        finish_keys(
            RING - BACK + j,
            halo_in[0, rows].astype(jnp.float32),
            halo_in[1, rows].astype(jnp.float32),
        )
        return carry

    lax.fori_loop(0, BACK, last_keys, 0)

    for offset in order:
        for i in range(2):
            send_keys(i, offset).wait_send()
            send_queries(i, offset).wait_send()
        send_dots(offset).wait_send()

    @pl.when(has_next)
    def _():
        for j in range(BACK):
            for i in range(2):
                send_halo(i, j).wait_send()

    @pl.when(has_prev)
    def _():
        for j in range(BACK):
            for i in range(2):
                send_back(i, j).wait_send()

    def drain(j, carry):
        for kind in range(3):
            remote, _ = send_out(kind, j)

            @pl.when(j != z)
            def _(remote=remote):
                remote.wait_send()

            out, width = ((gq_ref, PAIR), (gk_ref, HEAD_DIM), (gv_ref, HEAD_DIM))[kind]
            landed = out.at[:, cols_of(j, width)]
            pltpu.make_async_copy(landed, landed, out_recv.at[kind, j]).wait()
        return carry

    lax.fori_loop(0, RING, drain, 0)


def place(*refs):
    ins, outs, bufs, get, put = refs[:3], refs[3:6], refs[6:9], refs[9], refs[10]
    parts = [(i, j) for j in range(4) for i in range(3)]

    def step(i, j, out):
        rows = pl.ds(j * (ROWS // 4), ROWS // 4)
        src, dst, sems = (bufs[i], outs[i], put) if out else (ins[i], bufs[i], get)
        return pltpu.make_async_copy(src.at[rows], dst.at[rows], sems.at[i, j])

    for i, j in parts:
        step(i, j, False).start()
    for i, j in parts:
        step(i, j, False).wait()
        step(i, j, True).start()
    for i, j in parts:
        step(i, j, True).wait()


def per_device(halves, query_in, key_in, value_in, grad_out, row_dot, segments):
    here = pl.BlockSpec(memory_space=pl.ANY)
    low, wide = jnp.bfloat16, jnp.float32
    outs = tuple(jax.ShapeDtypeStruct(a.shape, low) for a in (query_in, key_in, value_in))
    blocks = segments.reshape(halves, RING, ROWS)
    sem = pltpu.SemaphoreType.DMA
    tokens, reach = RING * ROWS, (RING + BACK) * ROWS
    flops = 5 * 2 * RING * SPAN * 2 * ROWS * HEAD_DIM
    grads = pl.pallas_call(
        functools.partial(kernel, halves),
        out_shape=outs,
        in_specs=[here] * 6,
        out_specs=(here,) * 3,
        scratch_shapes=[
            pltpu.VMEM((tokens, PAIR), low),
            pltpu.VMEM((tokens, PAIR), low),
            pltpu.VMEM((reach, HEAD_DIM), low),
            pltpu.VMEM((reach, HEAD_DIM), low),
            pltpu.VMEM((HEAD_DIM, reach), low),
            pltpu.VMEM((2 * RING, ROWS), low),
            pltpu.VMEM((RING, 8, ROWS), wide),
            pltpu.VMEM((RING, 8, ROWS), wide),
            pltpu.VMEM((2, RING, ROWS), jnp.int32),
            pltpu.VMEM((RING, 8, ROWS), jnp.int32),
            pltpu.VMEM((reach, HEAD_DIM), wide),
            pltpu.VMEM((reach, HEAD_DIM), wide),
            pltpu.VMEM((tokens, PAIR), low),
            pltpu.VMEM((2, tokens, HEAD_DIM), low),
            pltpu.VMEM((2, BACK * ROWS, HEAD_DIM), low),
            pltpu.VMEM((2, BACK * ROWS, HEAD_DIM), low),
            sem((2, RING)), sem((2, RING)), sem((RING,)),
            sem((2, RING)), sem((2, RING)), sem((RING,)), sem((3,)),
            sem((2, BACK)), sem((2, BACK)), sem((2, BACK)), sem((2, BACK)),
            sem((3, RING)), sem((3, RING)),
        ],
        compiler_params=pltpu.CompilerParams(
            collective_id=0, has_side_effects=True, vmem_limit_bytes=62 * 1024 * 1024
        ),
        cost_estimate=pl.CostEstimate(
            flops=flops, bytes_accessed=5 << 20, transcendentals=2 * RING * SPAN * 2 * ROWS
        ),
        name="window_backward",
    )(query_in, key_in, value_in, grad_out, row_dot.T, blocks)
    return pl.pallas_call(
        place,
        out_shape=outs,
        in_specs=[here] * 3,
        out_specs=(here,) * 3,
        scratch_shapes=[pltpu.VMEM(o.shape, low) for o in outs] + [sem((3, 4))] * 2,
        name="place",
    )(*grads)


def solution(mesh):
    rows = P(("blk", "uly"), None)
    halves = mesh.shape["blk"] * mesh.shape["uly"] // RING
    return jax.shard_map(
        functools.partial(per_device, halves),
        mesh=mesh,
        in_specs=(rows,) * 5 + (P(),),
        out_specs=(rows,) * 3,
        check_vma=False,
    )
```

```python
import functools

import jax
import jax.numpy as jnp
from jax import lax
from jax.experimental import pallas as pl
from jax.experimental.pallas import tpu as pltpu
from jax.sharding import PartitionSpec as P

HEAD_DIM = 256
WINDOW = 512
LEAD = 3
ORDER = (1, 7, 2, 6, 3, 5, 4)
SCORE_SCALE = 0.0625
SOFT_CAP = 50.0
RING = 8
ROWS = 128
BACK = WINDOW // ROWS
SPAN = (BACK + 1) * ROWS
PAIR = 2 * HEAD_DIM
MESH = pl.DeviceIdType.MESH


def rows_of(index, count=1):
    return pl.ds(pl.multiple_of(index * ROWS, ROWS), count * ROWS)


def cols_of(index, width):
    return pl.ds(pl.multiple_of(index * width, width), width)


def kernel(
    halves,
    query_ref, key_ref, value_ref, grad_ref, dots_ref, seg_ref,
    gq_ref, gk_ref, gv_ref,
    q_buf, d_buf, k_buf, v_buf, kt_buf, dots_buf, r_src, r_buf, seg_buf, low_buf,
    k_acc, v_acc, gq_buf, gkv_buf, halo_out, halo_in,
    send_kv, send_qd, send_r, recv_kv, recv_qd, recv_r, seg_sem,
    halo_send, halo_recv, back_send, back_recv,
    out_send, out_recv, ring_sem, halo_sem,
):
    blk, uly = lax.axis_index("blk"), lax.axis_index("uly")
    side, z = uly // RING, lax.rem(uly, RING)
    half = blk * 2 + side
    has_prev, has_next = half > 0, half < halves - 1

    def device(h, zz):
        return (h // 2, lax.rem(h, 2) * RING + zz)

    def peer_of(offset):
        return lax.rem(z + offset, RING)

    prev_dev, next_dev = device(half - 1, z), device(half + 1, z)

    barrier = pltpu.get_barrier_semaphore()
    lead = z == LEAD

    def ring_signal(sem, offset):
        pl.semaphore_signal(
            sem, inc=1, device_id=device(half, peer_of(offset)), device_id_type=MESH
        )

    for offset in range(1, RING):

        @pl.when(peer_of(offset) != LEAD)
        def _(offset=offset):
            ring_signal(barrier, offset)

    def key_copy(i):
        src, buf = ((key_ref, k_buf), (value_ref, v_buf))[i]
        return pltpu.make_async_copy(
            src.at[:, cols_of(z, HEAD_DIM)], buf.at[rows_of(BACK + z)], recv_kv.at[i, z]
        )

    def query_copy(i):
        src, buf = ((query_ref, q_buf), (grad_ref, d_buf))[i]
        return pltpu.make_async_copy(
            src.at[:, cols_of(z, PAIR)], buf.at[rows_of(z)], recv_qd.at[i, z]
        )

    for i in range(2):
        key_copy(i).start()
        query_copy(i).start()
    own_seg = pltpu.make_async_copy(seg_ref.at[half], seg_buf.at[1], seg_sem.at[1])
    own_seg.start()
    dots_copy = pltpu.make_async_copy(dots_ref, dots_buf, seg_sem.at[2])
    dots_copy.start()

    @pl.when(has_prev)
    def _():
        pltpu.make_async_copy(seg_ref.at[half - 1], seg_buf.at[0], seg_sem.at[0]).start()

    dots_copy.wait()
    turned = dots_buf[...].astype(jnp.float32)
    for p in range(RING):
        r_src[p] = jnp.concatenate(
            [turned[2 * p : 2 * p + 2], jnp.zeros((6, ROWS), jnp.float32)], axis=0
        )
    r_buf[z] = r_src[z]

    @pl.when(jnp.logical_not(lead))
    def _():
        pl.semaphore_wait(barrier, RING - 1)
        pl.semaphore_signal(ring_sem, inc=1, device_id=device(half, LEAD), device_id_type=MESH)

    @pl.when(lead)
    def _():
        pl.semaphore_wait(ring_sem, RING - 1)

        @pl.when(has_prev)
        def _():
            pl.semaphore_signal(barrier, inc=1, device_id=prev_dev, device_id_type=MESH)

        @pl.when(has_next)
        def _():
            pl.semaphore_signal(barrier, inc=1, device_id=next_dev, device_id_type=MESH)

    def send(src, dst, send_sem, recv_sem, dev):
        return pltpu.make_async_remote_copy(
            src_ref=src, dst_ref=dst, send_sem=send_sem, recv_sem=recv_sem,
            device_id=dev, device_id_type=MESH,
        )

    def send_keys(i, offset):
        src, buf = ((key_ref, k_buf), (value_ref, v_buf))[i]
        p = peer_of(offset)
        return send(
            src.at[:, cols_of(p, HEAD_DIM)], buf.at[rows_of(BACK + z)],
            send_kv.at[i, offset], recv_kv.at[i, z], device(half, p),
        )

    def send_queries(i, offset):
        src, buf = ((query_ref, q_buf), (grad_ref, d_buf))[i]
        p = peer_of(offset)
        return send(
            src.at[:, cols_of(p, PAIR)], buf.at[rows_of(z)],
            send_qd.at[i, offset], recv_qd.at[i, z], device(half, p),
        )

    def send_dots(offset):
        p = peer_of(offset)
        return send(
            r_src.at[p, :2], r_buf.at[z, :2], send_r.at[offset], recv_r.at[z], device(half, p)
        )

    order = ORDER
    for offset in order:
        for i in range(2):
            send_keys(i, offset).start()
    for offset in order:
        send_dots(offset).start()
        for i in range(2):
            send_queries(i, offset).start()

    own_seg.wait()

    @pl.when(has_prev)
    def _():
        pltpu.make_async_copy(seg_ref.at[half], seg_buf.at[0], seg_sem.at[0]).wait()

    @pl.when(jnp.logical_not(has_prev))
    def _():
        seg_buf[0] = jnp.full((RING, ROWS), -1, jnp.int32)
        k_buf[: BACK * ROWS] = jnp.zeros((BACK * ROWS, HEAD_DIM), jnp.bfloat16)
        v_buf[: BACK * ROWS] = jnp.zeros((BACK * ROWS, HEAD_DIM), jnp.bfloat16)

    before, here = seg_buf[0], seg_buf[1]
    first = jnp.zeros((RING, ROWS), jnp.int32)
    for doc in range(16):
        below = jnp.sum(
            (before < doc).astype(jnp.int32) + (here < doc).astype(jnp.int32),
            keepdims=True,
        )
        first = jnp.where(here == doc, below, first)
    tile_of = lax.broadcasted_iota(jnp.int32, (RING, ROWS), 0)
    lane_of = lax.broadcasted_iota(jnp.int32, (RING, ROWS), 1)
    origin = (RING - BACK) * ROWS + tile_of * ROWS
    low = jnp.maximum(first - origin, lane_of + 1)
    for t in range(RING):
        low_buf[t] = jnp.broadcast_to(low[t : t + 1], (8, ROWS))

    k_acc[...] = jnp.zeros(k_acc.shape, jnp.float32)
    v_acc[...] = jnp.zeros(v_acc.shape, jnp.float32)

    def wait_keys(j):
        key_slot, value_slot = k_buf.at[rows_of(BACK + j)], v_buf.at[rows_of(BACK + j)]
        pltpu.make_async_copy(key_slot, key_slot, recv_kv.at[0, j]).wait()
        pltpu.make_async_copy(value_slot, value_slot, recv_kv.at[1, j]).wait()

    def turn_keys(index):
        kt_buf[:, rows_of(index)] = k_buf[rows_of(index)].T

    def send_halo(i, j):
        buf = (k_buf, v_buf)[i]
        return send(
            buf.at[rows_of(RING + j)], buf.at[rows_of(j)],
            halo_send.at[i, j], halo_recv.at[i, j], next_dev,
        )

    @pl.when(lead)
    def _():
        pl.semaphore_wait(barrier, has_prev.astype(jnp.int32) + has_next.astype(jnp.int32))
        for offset in range(1, RING):
            ring_signal(halo_sem, offset)

    @pl.when(jnp.logical_not(lead))
    def _():
        pl.semaphore_wait(halo_sem, 1)

    for j in range(BACK):
        wait_keys(RING - BACK + j)

        @pl.when(has_next)
        def _(j=j):
            send_halo(0, j).start()
            send_halo(1, j).start()

    def turn_late(j, carry):
        turn_keys(RING + j)
        return carry

    lax.fori_loop(0, BACK, turn_late, 0)

    def take_early(j, carry):
        wait_keys(j)
        turn_keys(BACK + j)
        return carry

    lax.fori_loop(0, RING - BACK, take_early, 0)

    @pl.when(has_prev)
    def _():
        for j in range(BACK):
            for i in range(2):
                slot = (k_buf, v_buf)[i].at[rows_of(j)]
                pltpu.make_async_copy(slot, slot, halo_recv.at[i, j]).wait()

    def turn_halo(j, carry):
        turn_keys(j)
        return carry

    lax.fori_loop(0, BACK, turn_halo, 0)

    def send_out(kind, j):
        buf, out, width = (
            (gq_buf.at[rows_of(j)], gq_ref, PAIR),
            (gkv_buf.at[0, rows_of(j)], gk_ref, HEAD_DIM),
            (gkv_buf.at[1, rows_of(j)], gv_ref, HEAD_DIM),
        )[kind]
        dst = out.at[:, cols_of(z, width)]
        remote = send(buf, dst, out_send.at[kind, j], out_recv.at[kind, z], device(half, j))
        local = pltpu.make_async_copy(buf, dst, out_recv.at[kind, z])
        return remote, local

    def start_out(kind, j):
        remote, local = send_out(kind, j)

        @pl.when(j != z)
        def _():
            remote.start()

        @pl.when(j == z)
        def _():
            local.start()

    def nt_dot(a, b):
        return lax.dot_general(
            a, b, (((1,), (1,)), ((), ())), preferred_element_type=jnp.float32
        )

    def dot(a, b):
        return jnp.dot(a, b, preferred_element_type=jnp.float32)

    def finish_keys(j, extra_key, extra_value):
        rows = rows_of(BACK + j)
        gkv_buf[0, rows_of(j)] = (
            (k_acc[rows] * SCORE_SCALE + extra_key).astype(jnp.bfloat16)
        )
        gkv_buf[1, rows_of(j)] = (v_acc[rows] + extra_value).astype(jnp.bfloat16)
        start_out(1, j)
        start_out(2, j)

    def tile(t, carry):
        for i in range(2):
            slot = (q_buf, d_buf)[i].at[rows_of(t)]
            pltpu.make_async_copy(slot, slot, recv_qd.at[i, t]).wait()

        @pl.when(t != z)
        def _():
            pltpu.make_async_copy(r_buf.at[t, :2], r_buf.at[t, :2], recv_r.at[t]).wait()

        span = rows_of(t, BACK + 1)
        queries, grads = q_buf[rows_of(t)], d_buf[rows_of(t)]
        queries = jnp.concatenate([queries[:, :HEAD_DIM], queries[:, HEAD_DIM:]], axis=0)
        grads = jnp.concatenate([grads[:, :HEAD_DIM], grads[:, HEAD_DIM:]], axis=0)
        sums = r_buf[t]
        sums = jnp.concatenate([sums[0:1], sums[1:2]], axis=1)
        least = low_buf[t][0:1]
        least = jnp.concatenate([least, least], axis=1)
        keys = k_buf[span]
        bent = jnp.tanh(nt_dot(keys, queries) * (SCORE_SCALE / SOFT_CAP))
        place = lax.broadcasted_iota(jnp.int32, (SPAN, 2 * ROWS), 0)
        column = lax.broadcasted_iota(jnp.int32, (SPAN, 2 * ROWS), 1)
        most = WINDOW + jnp.where(column < ROWS, column, column - ROWS)
        allowed = (place >= least) & (place <= most)
        weight = jnp.where(allowed, jnp.exp(SOFT_CAP * bent), 0.0)
        prob = weight * (1.0 / jnp.sum(weight, axis=0, keepdims=True))
        grad_prob = nt_dot(v_buf[span], grads)
        grad_score = (prob * (grad_prob - sums) * (1.0 - bent * bent)).astype(jnp.bfloat16)
        v_acc[span] += dot(prob.astype(jnp.bfloat16), grads)
        k_acc[span] += dot(grad_score, queries)
        turned_grad = dot(kt_buf[:, span], grad_score)
        query_grad = (turned_grad * SCORE_SCALE).T.astype(jnp.bfloat16)
        gq_buf[rows_of(t), :HEAD_DIM] = query_grad[:ROWS]
        gq_buf[rows_of(t), HEAD_DIM:] = query_grad[ROWS:]
        start_out(0, t)
        return carry

    def send_back(i, j):
        return send(
            halo_out.at[i, rows_of(j)], halo_in.at[i, rows_of(j)],
            back_send.at[i, j], back_recv.at[i, j], prev_dev,
        )

    def step_of(t):
        ahead, at = lax.rem(t - z + RING, RING), 0
        for step, offset in enumerate(order, 1):
            at = jnp.where(ahead == RING - offset, step, at)
        return at

    def done_at(first, last):
        at = step_of(first)
        for t in range(first + 1, last + 1):
            at = jnp.maximum(at, step_of(t))
        return at

    halo_done = [done_at(0, j) for j in range(BACK)]
    own_done = [done_at(j, j + BACK) for j in range(RING - BACK)]

    def one_step(step, carry):
        ahead = 0
        for at, offset in enumerate(order, 1):
            ahead = jnp.where(step == at, RING - offset, ahead)
        t = lax.rem(z + ahead, RING)
        tile(t, carry)
        for j in range(BACK):

            @pl.when((halo_done[j] == step) & has_prev)
            def _(j=j):
                rows = rows_of(j)
                halo_out[0, rows] = (k_acc[rows] * SCORE_SCALE).astype(jnp.bfloat16)
                halo_out[1, rows] = v_acc[rows].astype(jnp.bfloat16)
                send_back(0, j).start()
                send_back(1, j).start()

        return carry

    lax.fori_loop(0, RING, one_step, 0)

    def first_keys(j, carry):
        finish_keys(j, 0.0, 0.0)
        return carry

    lax.fori_loop(0, RING - BACK, first_keys, 0)

    @pl.when(jnp.logical_not(has_next))
    def _():
        halo_in[...] = jnp.zeros(halo_in.shape, jnp.bfloat16)

    def last_keys(j, carry):
        rows = rows_of(j)

        @pl.when(has_next)
        def _():
            for i in range(2):
                slot = halo_in.at[i, rows]
                pltpu.make_async_copy(slot, slot, back_recv.at[i, j]).wait()

        finish_keys(
            RING - BACK + j,
            halo_in[0, rows].astype(jnp.float32),
            halo_in[1, rows].astype(jnp.float32),
        )
        return carry

    lax.fori_loop(0, BACK, last_keys, 0)

    for offset in order:
        for i in range(2):
            send_keys(i, offset).wait_send()
            send_queries(i, offset).wait_send()
        send_dots(offset).wait_send()

    @pl.when(has_next)
    def _():
        for j in range(BACK):
            for i in range(2):
                send_halo(i, j).wait_send()

    @pl.when(has_prev)
    def _():
        for j in range(BACK):
            for i in range(2):
                send_back(i, j).wait_send()

    def drain(j, carry):
        for kind in range(3):
            remote, _ = send_out(kind, j)

            @pl.when(j != z)
            def _(remote=remote):
                remote.wait_send()

            out, width = ((gq_ref, PAIR), (gk_ref, HEAD_DIM), (gv_ref, HEAD_DIM))[kind]
            landed = out.at[:, cols_of(j, width)]
            pltpu.make_async_copy(landed, landed, out_recv.at[kind, j]).wait()
        return carry

    lax.fori_loop(0, RING, drain, 0)


def place(*refs):
    ins, outs, bufs, get, put = refs[:3], refs[3:6], refs[6:9], refs[9], refs[10]
    parts = [(i, j) for j in range(4) for i in range(3)]

    def step(i, j, out):
        rows = pl.ds(j * (ROWS // 4), ROWS // 4)
        src, dst, sems = (bufs[i], outs[i], put) if out else (ins[i], bufs[i], get)
        return pltpu.make_async_copy(src.at[rows], dst.at[rows], sems.at[i, j])

    for i, j in parts:
        step(i, j, False).start()
    for i, j in parts:
        step(i, j, False).wait()
        step(i, j, True).start()
    for i, j in parts:
        step(i, j, True).wait()


def per_device(halves, query_in, key_in, value_in, grad_out, row_dot, segments):
    here = pl.BlockSpec(memory_space=pl.ANY)
    low, wide = jnp.bfloat16, jnp.float32
    outs = tuple(jax.ShapeDtypeStruct(a.shape, low) for a in (query_in, key_in, value_in))
    blocks = segments.reshape(halves, RING, ROWS)
    sem = pltpu.SemaphoreType.DMA
    tokens, reach = RING * ROWS, (RING + BACK) * ROWS
    flops = 5 * 2 * RING * SPAN * 2 * ROWS * HEAD_DIM
    grads = pl.pallas_call(
        functools.partial(kernel, halves),
        out_shape=outs,
        in_specs=[here] * 6,
        out_specs=(here,) * 3,
        scratch_shapes=[
            pltpu.VMEM((tokens, PAIR), low),
            pltpu.VMEM((tokens, PAIR), low),
            pltpu.VMEM((reach, HEAD_DIM), low),
            pltpu.VMEM((reach, HEAD_DIM), low),
            pltpu.VMEM((HEAD_DIM, reach), low),
            pltpu.VMEM((2 * RING, ROWS), low),
            pltpu.VMEM((RING, 8, ROWS), wide),
            pltpu.VMEM((RING, 8, ROWS), wide),
            pltpu.VMEM((2, RING, ROWS), jnp.int32),
            pltpu.VMEM((RING, 8, ROWS), jnp.int32),
            pltpu.VMEM((reach, HEAD_DIM), wide),
            pltpu.VMEM((reach, HEAD_DIM), wide),
            pltpu.VMEM((tokens, PAIR), low),
            pltpu.VMEM((2, tokens, HEAD_DIM), low),
            pltpu.VMEM((2, BACK * ROWS, HEAD_DIM), low),
            pltpu.VMEM((2, BACK * ROWS, HEAD_DIM), low),
            sem((2, RING)), sem((2, RING)), sem((RING,)),
            sem((2, RING)), sem((2, RING)), sem((RING,)), sem((3,)),
            sem((2, BACK)), sem((2, BACK)), sem((2, BACK)), sem((2, BACK)),
            sem((3, RING)), sem((3, RING)),
            pltpu.SemaphoreType.REGULAR, pltpu.SemaphoreType.REGULAR,
        ],
        compiler_params=pltpu.CompilerParams(
            collective_id=0, has_side_effects=True, vmem_limit_bytes=62 * 1024 * 1024
        ),
        cost_estimate=pl.CostEstimate(
            flops=flops, bytes_accessed=5 << 20, transcendentals=2 * RING * SPAN * 2 * ROWS
        ),
        name="window_backward",
    )(query_in, key_in, value_in, grad_out, row_dot.T, blocks)
    return pl.pallas_call(
        place,
        out_shape=outs,
        in_specs=[here] * 3,
        out_specs=(here,) * 3,
        scratch_shapes=[pltpu.VMEM(o.shape, low) for o in outs] + [sem((3, 4))] * 2,
        name="place",
    )(*grads)


def solution(mesh):
    rows = P(("blk", "uly"), None)
    halves = mesh.shape["blk"] * mesh.shape["uly"] // RING
    return jax.shard_map(
        functools.partial(per_device, halves),
        mesh=mesh,
        in_specs=(rows,) * 5 + (P(),),
        out_specs=(rows,) * 3,
        check_vma=False,
    )
```

```python
import functools

import jax
import jax.numpy as jnp
from jax import lax
from jax.experimental import pallas as pl
from jax.experimental.pallas import tpu as pltpu
from jax.sharding import PartitionSpec as P

HEAD_DIM = 256
WINDOW = 512
LEAD = 3
ORDER = (1, 7, 4, 3, 5, 2, 6)
SCORE_SCALE = 0.0625
SOFT_CAP = 50.0
RING = 8
ROWS = 128
BACK = WINDOW // ROWS
SPAN = (BACK + 1) * ROWS
PAIR = 2 * HEAD_DIM
MESH = pl.DeviceIdType.MESH


def rows_of(index, count=1):
    return pl.ds(pl.multiple_of(index * ROWS, ROWS), count * ROWS)


def cols_of(index, width):
    return pl.ds(pl.multiple_of(index * width, width), width)


def kernel(
    halves,
    query_ref, key_ref, value_ref, grad_ref, dots_ref, seg_ref,
    gq_ref, gk_ref, gv_ref,
    q_buf, d_buf, k_buf, v_buf, kt_buf, dots_buf, r_src, r_buf, seg_buf, low_buf,
    k_acc, v_acc, gq_buf, gkv_buf, halo_out, halo_in,
    send_kv, send_qd, send_r, recv_kv, recv_qd, recv_r, seg_sem,
    halo_send, halo_recv, back_send, back_recv,
    out_send, out_recv, ring_sem, halo_sem,
):
    blk, uly = lax.axis_index("blk"), lax.axis_index("uly")
    side, z = uly // RING, lax.rem(uly, RING)
    half = blk * 2 + side
    has_prev, has_next = half > 0, half < halves - 1

    def device(h, zz):
        return (h // 2, lax.rem(h, 2) * RING + zz)

    def peer_of(offset):
        return lax.rem(z + offset, RING)

    prev_dev, next_dev = device(half - 1, z), device(half + 1, z)

    barrier = pltpu.get_barrier_semaphore()
    lead = z == LEAD

    def ring_signal(sem, offset):
        pl.semaphore_signal(
            sem, inc=1, device_id=device(half, peer_of(offset)), device_id_type=MESH
        )

    for offset in range(1, RING):

        @pl.when(peer_of(offset) != LEAD)
        def _(offset=offset):
            ring_signal(barrier, offset)

    def key_copy(i):
        src, buf = ((key_ref, k_buf), (value_ref, v_buf))[i]
        return pltpu.make_async_copy(
            src.at[:, cols_of(z, HEAD_DIM)], buf.at[rows_of(BACK + z)], recv_kv.at[i, z]
        )

    def query_copy(i):
        src, buf = ((query_ref, q_buf), (grad_ref, d_buf))[i]
        return pltpu.make_async_copy(
            src.at[:, cols_of(z, PAIR)], buf.at[rows_of(z)], recv_qd.at[i, z]
        )

    for i in range(2):
        key_copy(i).start()
        query_copy(i).start()
    own_seg = pltpu.make_async_copy(seg_ref.at[half], seg_buf.at[1], seg_sem.at[1])
    own_seg.start()
    dots_copy = pltpu.make_async_copy(dots_ref, dots_buf, seg_sem.at[2])
    dots_copy.start()

    @pl.when(has_prev)
    def _():
        pltpu.make_async_copy(seg_ref.at[half - 1], seg_buf.at[0], seg_sem.at[0]).start()

    dots_copy.wait()
    turned = dots_buf[...].astype(jnp.float32)
    for p in range(RING):
        r_src[p] = jnp.concatenate(
            [turned[2 * p : 2 * p + 2], jnp.zeros((6, ROWS), jnp.float32)], axis=0
        )
    r_buf[z] = r_src[z]

    @pl.when(jnp.logical_not(lead))
    def _():
        pl.semaphore_wait(barrier, RING - 1)
        pl.semaphore_signal(ring_sem, inc=1, device_id=device(half, LEAD), device_id_type=MESH)

    @pl.when(lead)
    def _():
        pl.semaphore_wait(ring_sem, RING - 1)

        @pl.when(has_prev)
        def _():
            pl.semaphore_signal(barrier, inc=1, device_id=prev_dev, device_id_type=MESH)

        @pl.when(has_next)
        def _():
            pl.semaphore_signal(barrier, inc=1, device_id=next_dev, device_id_type=MESH)

    def send(src, dst, send_sem, recv_sem, dev):
        return pltpu.make_async_remote_copy(
            src_ref=src, dst_ref=dst, send_sem=send_sem, recv_sem=recv_sem,
            device_id=dev, device_id_type=MESH,
        )

    def send_keys(i, offset):
        src, buf = ((key_ref, k_buf), (value_ref, v_buf))[i]
        p = peer_of(offset)
        return send(
            src.at[:, cols_of(p, HEAD_DIM)], buf.at[rows_of(BACK + z)],
            send_kv.at[i, offset], recv_kv.at[i, z], device(half, p),
        )

    def send_queries(i, offset):
        src, buf = ((query_ref, q_buf), (grad_ref, d_buf))[i]
        p = peer_of(offset)
        return send(
            src.at[:, cols_of(p, PAIR)], buf.at[rows_of(z)],
            send_qd.at[i, offset], recv_qd.at[i, z], device(half, p),
        )

    def send_dots(offset):
        p = peer_of(offset)
        return send(
            r_src.at[p, :2], r_buf.at[z, :2], send_r.at[offset], recv_r.at[z], device(half, p)
        )

    order = ORDER
    for offset in order:
        for i in range(2):
            send_keys(i, offset).start()
    for offset in order:
        send_dots(offset).start()
        for i in range(2):
            send_queries(i, offset).start()

    own_seg.wait()

    @pl.when(has_prev)
    def _():
        pltpu.make_async_copy(seg_ref.at[half], seg_buf.at[0], seg_sem.at[0]).wait()

    @pl.when(jnp.logical_not(has_prev))
    def _():
        seg_buf[0] = jnp.full((RING, ROWS), -1, jnp.int32)
        k_buf[: BACK * ROWS] = jnp.zeros((BACK * ROWS, HEAD_DIM), jnp.bfloat16)
        v_buf[: BACK * ROWS] = jnp.zeros((BACK * ROWS, HEAD_DIM), jnp.bfloat16)

    before, here = seg_buf[0], seg_buf[1]
    first = jnp.zeros((RING, ROWS), jnp.int32)
    for doc in range(16):
        below = jnp.sum(
            (before < doc).astype(jnp.int32) + (here < doc).astype(jnp.int32),
            keepdims=True,
        )
        first = jnp.where(here == doc, below, first)
    tile_of = lax.broadcasted_iota(jnp.int32, (RING, ROWS), 0)
    lane_of = lax.broadcasted_iota(jnp.int32, (RING, ROWS), 1)
    origin = (RING - BACK) * ROWS + tile_of * ROWS
    low = jnp.maximum(first - origin, lane_of + 1)
    for t in range(RING):
        low_buf[t] = jnp.broadcast_to(low[t : t + 1], (8, ROWS))

    k_acc[...] = jnp.zeros(k_acc.shape, jnp.float32)
    v_acc[...] = jnp.zeros(v_acc.shape, jnp.float32)

    def wait_keys(j):
        key_slot, value_slot = k_buf.at[rows_of(BACK + j)], v_buf.at[rows_of(BACK + j)]
        pltpu.make_async_copy(key_slot, key_slot, recv_kv.at[0, j]).wait()
        pltpu.make_async_copy(value_slot, value_slot, recv_kv.at[1, j]).wait()

    def turn_keys(index):
        kt_buf[:, rows_of(index)] = k_buf[rows_of(index)].T

    def send_halo(i, j):
        buf = (k_buf, v_buf)[i]
        return send(
            buf.at[rows_of(RING + j)], buf.at[rows_of(j)],
            halo_send.at[i, j], halo_recv.at[i, j], next_dev,
        )

    @pl.when(lead)
    def _():
        pl.semaphore_wait(barrier, has_prev.astype(jnp.int32) + has_next.astype(jnp.int32))
        for offset in range(1, RING):
            ring_signal(halo_sem, offset)

    @pl.when(jnp.logical_not(lead))
    def _():
        pl.semaphore_wait(halo_sem, 1)

    for j in range(BACK):
        wait_keys(RING - BACK + j)

        @pl.when(has_next)
        def _(j=j):
            send_halo(0, j).start()
            send_halo(1, j).start()

    def turn_late(j, carry):
        turn_keys(RING + j)
        return carry

    lax.fori_loop(0, BACK, turn_late, 0)

    def take_early(j, carry):
        wait_keys(j)
        turn_keys(BACK + j)
        return carry

    lax.fori_loop(0, RING - BACK, take_early, 0)

    @pl.when(has_prev)
    def _():
        for j in range(BACK):
            for i in range(2):
                slot = (k_buf, v_buf)[i].at[rows_of(j)]
                pltpu.make_async_copy(slot, slot, halo_recv.at[i, j]).wait()

    def turn_halo(j, carry):
        turn_keys(j)
        return carry

    lax.fori_loop(0, BACK, turn_halo, 0)

    def send_out(kind, j):
        buf, out, width = (
            (gq_buf.at[rows_of(j)], gq_ref, PAIR),
            (gkv_buf.at[0, rows_of(j)], gk_ref, HEAD_DIM),
            (gkv_buf.at[1, rows_of(j)], gv_ref, HEAD_DIM),
        )[kind]
        dst = out.at[:, cols_of(z, width)]
        remote = send(buf, dst, out_send.at[kind, j], out_recv.at[kind, z], device(half, j))
        local = pltpu.make_async_copy(buf, dst, out_recv.at[kind, z])
        return remote, local

    def start_out(kind, j):
        remote, local = send_out(kind, j)

        @pl.when(j != z)
        def _():
            remote.start()

        @pl.when(j == z)
        def _():
            local.start()

    def nt_dot(a, b):
        return lax.dot_general(
            a, b, (((1,), (1,)), ((), ())), preferred_element_type=jnp.float32
        )

    def dot(a, b):
        return jnp.dot(a, b, preferred_element_type=jnp.float32)

    def finish_keys(j, extra_key, extra_value):
        rows = rows_of(BACK + j)
        gkv_buf[0, rows_of(j)] = (
            (k_acc[rows] * SCORE_SCALE + extra_key).astype(jnp.bfloat16)
        )
        gkv_buf[1, rows_of(j)] = (v_acc[rows] + extra_value).astype(jnp.bfloat16)
        start_out(1, j)
        start_out(2, j)

    def tile(t, carry):
        for i in range(2):
            slot = (q_buf, d_buf)[i].at[rows_of(t)]
            pltpu.make_async_copy(slot, slot, recv_qd.at[i, t]).wait()

        @pl.when(t != z)
        def _():
            pltpu.make_async_copy(r_buf.at[t, :2], r_buf.at[t, :2], recv_r.at[t]).wait()

        span = rows_of(t, BACK + 1)
        queries, grads = q_buf[rows_of(t)], d_buf[rows_of(t)]
        queries = jnp.concatenate([queries[:, :HEAD_DIM], queries[:, HEAD_DIM:]], axis=0)
        grads = jnp.concatenate([grads[:, :HEAD_DIM], grads[:, HEAD_DIM:]], axis=0)
        sums = r_buf[t]
        sums = jnp.concatenate([sums[0:1], sums[1:2]], axis=1)
        least = low_buf[t][0:1]
        least = jnp.concatenate([least, least], axis=1)
        keys = k_buf[span]
        bent = jnp.tanh(nt_dot(keys, queries) * (SCORE_SCALE / SOFT_CAP))
        place = lax.broadcasted_iota(jnp.int32, (SPAN, 2 * ROWS), 0)
        column = lax.broadcasted_iota(jnp.int32, (SPAN, 2 * ROWS), 1)
        most = WINDOW + jnp.where(column < ROWS, column, column - ROWS)
        allowed = (place >= least) & (place <= most)
        weight = jnp.where(allowed, jnp.exp(SOFT_CAP * bent), 0.0)
        prob = weight * (1.0 / jnp.sum(weight, axis=0, keepdims=True))
        grad_prob = nt_dot(v_buf[span], grads)
        grad_score = (prob * (grad_prob - sums) * (1.0 - bent * bent)).astype(jnp.bfloat16)
        v_acc[span] += dot(prob.astype(jnp.bfloat16), grads)
        k_acc[span] += dot(grad_score, queries)
        turned_grad = dot(kt_buf[:, span], grad_score)
        query_grad = (turned_grad * SCORE_SCALE).T.astype(jnp.bfloat16)
        gq_buf[rows_of(t), :HEAD_DIM] = query_grad[:ROWS]
        gq_buf[rows_of(t), HEAD_DIM:] = query_grad[ROWS:]
        start_out(0, t)
        return carry

    def send_back(i, j):
        return send(
            halo_out.at[i, rows_of(j)], halo_in.at[i, rows_of(j)],
            back_send.at[i, j], back_recv.at[i, j], prev_dev,
        )

    def step_of(t):
        ahead, at = lax.rem(t - z + RING, RING), 0
        for step, offset in enumerate(order, 1):
            at = jnp.where(ahead == RING - offset, step, at)
        return at

    def done_at(first, last):
        at = step_of(first)
        for t in range(first + 1, last + 1):
            at = jnp.maximum(at, step_of(t))
        return at

    halo_done = [done_at(0, j) for j in range(BACK)]
    own_done = [done_at(j, j + BACK) for j in range(RING - BACK)]

    def one_step(step, carry):
        ahead = 0
        for at, offset in enumerate(order, 1):
            ahead = jnp.where(step == at, RING - offset, ahead)
        t = lax.rem(z + ahead, RING)
        tile(t, carry)
        for j in range(BACK):

            @pl.when((halo_done[j] == step) & has_prev)
            def _(j=j):
                rows = rows_of(j)
                halo_out[0, rows] = (k_acc[rows] * SCORE_SCALE).astype(jnp.bfloat16)
                halo_out[1, rows] = v_acc[rows].astype(jnp.bfloat16)
                send_back(0, j).start()
                send_back(1, j).start()

        return carry

    lax.fori_loop(0, RING, one_step, 0)

    def first_keys(j, carry):
        finish_keys(j, 0.0, 0.0)
        return carry

    for j in (1, 0, 2, 3):
        first_keys(j, 0)

    @pl.when(jnp.logical_not(has_next))
    def _():
        halo_in[...] = jnp.zeros(halo_in.shape, jnp.bfloat16)

    def last_keys(j, carry):
        rows = rows_of(j)

        @pl.when(has_next)
        def _():
            for i in range(2):
                slot = halo_in.at[i, rows]
                pltpu.make_async_copy(slot, slot, back_recv.at[i, j]).wait()

        finish_keys(
            RING - BACK + j,
            halo_in[0, rows].astype(jnp.float32),
            halo_in[1, rows].astype(jnp.float32),
        )
        return carry

    lax.fori_loop(0, BACK, last_keys, 0)

    for offset in order:
        for i in range(2):
            send_keys(i, offset).wait_send()
            send_queries(i, offset).wait_send()
        send_dots(offset).wait_send()

    @pl.when(has_next)
    def _():
        for j in range(BACK):
            for i in range(2):
                send_halo(i, j).wait_send()

    @pl.when(has_prev)
    def _():
        for j in range(BACK):
            for i in range(2):
                send_back(i, j).wait_send()

    def drain(j, carry):
        for kind in range(3):
            remote, _ = send_out(kind, j)

            @pl.when(j != z)
            def _(remote=remote):
                remote.wait_send()

            out, width = ((gq_ref, PAIR), (gk_ref, HEAD_DIM), (gv_ref, HEAD_DIM))[kind]
            landed = out.at[:, cols_of(j, width)]
            pltpu.make_async_copy(landed, landed, out_recv.at[kind, j]).wait()
        return carry

    lax.fori_loop(0, RING, drain, 0)


def place(*refs):
    ins, outs, bufs, get, put = refs[:3], refs[3:6], refs[6:9], refs[9], refs[10]
    parts = [(i, j) for j in range(4) for i in range(3)]

    def step(i, j, out):
        rows = pl.ds(j * (ROWS // 4), ROWS // 4)
        src, dst, sems = (bufs[i], outs[i], put) if out else (ins[i], bufs[i], get)
        return pltpu.make_async_copy(src.at[rows], dst.at[rows], sems.at[i, j])

    for i, j in parts:
        step(i, j, False).start()
    for i, j in parts:
        step(i, j, False).wait()
        step(i, j, True).start()
    for i, j in parts:
        step(i, j, True).wait()


def per_device(halves, query_in, key_in, value_in, grad_out, row_dot, segments):
    here = pl.BlockSpec(memory_space=pl.ANY)
    low, wide = jnp.bfloat16, jnp.float32
    outs = tuple(jax.ShapeDtypeStruct(a.shape, low) for a in (query_in, key_in, value_in))
    blocks = segments.reshape(halves, RING, ROWS)
    sem = pltpu.SemaphoreType.DMA
    tokens, reach = RING * ROWS, (RING + BACK) * ROWS
    flops = 5 * 2 * RING * SPAN * 2 * ROWS * HEAD_DIM
    grads = pl.pallas_call(
        functools.partial(kernel, halves),
        out_shape=outs,
        in_specs=[here] * 6,
        out_specs=(here,) * 3,
        scratch_shapes=[
            pltpu.VMEM((tokens, PAIR), low),
            pltpu.VMEM((tokens, PAIR), low),
            pltpu.VMEM((reach, HEAD_DIM), low),
            pltpu.VMEM((reach, HEAD_DIM), low),
            pltpu.VMEM((HEAD_DIM, reach), low),
            pltpu.VMEM((2 * RING, ROWS), low),
            pltpu.VMEM((RING, 8, ROWS), wide),
            pltpu.VMEM((RING, 8, ROWS), wide),
            pltpu.VMEM((2, RING, ROWS), jnp.int32),
            pltpu.VMEM((RING, 8, ROWS), jnp.int32),
            pltpu.VMEM((reach, HEAD_DIM), wide),
            pltpu.VMEM((reach, HEAD_DIM), wide),
            pltpu.VMEM((tokens, PAIR), low),
            pltpu.VMEM((2, tokens, HEAD_DIM), low),
            pltpu.VMEM((2, BACK * ROWS, HEAD_DIM), low),
            pltpu.VMEM((2, BACK * ROWS, HEAD_DIM), low),
            sem((2, RING)), sem((2, RING)), sem((RING,)),
            sem((2, RING)), sem((2, RING)), sem((RING,)), sem((3,)),
            sem((2, BACK)), sem((2, BACK)), sem((2, BACK)), sem((2, BACK)),
            sem((3, RING)), sem((3, RING)),
            pltpu.SemaphoreType.REGULAR, pltpu.SemaphoreType.REGULAR,
        ],
        compiler_params=pltpu.CompilerParams(
            collective_id=0, has_side_effects=True, vmem_limit_bytes=62 * 1024 * 1024
        ),
        cost_estimate=pl.CostEstimate(
            flops=flops, bytes_accessed=5 << 20, transcendentals=2 * RING * SPAN * 2 * ROWS
        ),
        name="window_backward",
    )(query_in, key_in, value_in, grad_out, row_dot.T, blocks)
    return pl.pallas_call(
        place,
        out_shape=outs,
        in_specs=[here] * 3,
        out_specs=(here,) * 3,
        scratch_shapes=[pltpu.VMEM(o.shape, low) for o in outs] + [sem((3, 4))] * 2,
        name="place",
    )(*grads)


def solution(mesh):
    rows = P(("blk", "uly"), None)
    halves = mesh.shape["blk"] * mesh.shape["uly"] // RING
    return jax.shard_map(
        functools.partial(per_device, halves),
        mesh=mesh,
        in_specs=(rows,) * 5 + (P(),),
        out_specs=(rows,) * 3,
        check_vma=False,
    )
```

```python
import functools

import jax
import jax.numpy as jnp
from jax import lax
from jax.experimental import pallas as pl
from jax.experimental.pallas import tpu as pltpu
from jax.sharding import PartitionSpec as P

HEAD_DIM = 256
WINDOW = 512
LEAD = 3
ORDER = (1, 7, 4, 3, 5, 2, 6)
SCORE_SCALE = 0.0625
SOFT_CAP = 50.0
RING = 8
ROWS = 128
BACK = WINDOW // ROWS
SPAN = (BACK + 1) * ROWS
PAIR = 2 * HEAD_DIM
MESH = pl.DeviceIdType.MESH


def rows_of(index, count=1):
    return pl.ds(pl.multiple_of(index * ROWS, ROWS), count * ROWS)


def cols_of(index, width):
    return pl.ds(pl.multiple_of(index * width, width), width)


def kernel(
    halves,
    query_ref, key_ref, value_ref, grad_ref, dots_ref, seg_ref,
    gq_ref, gk_ref, gv_ref,
    q_buf, d_buf, k_buf, v_buf, kt_buf, dots_buf, r_src, r_buf, seg_buf, low_buf,
    k_acc, v_acc, gq_buf, gkv_buf, halo_out, halo_in,
    send_kv, send_qd, send_r, recv_kv, recv_qd, recv_r, seg_sem,
    halo_send, halo_recv, back_send, back_recv,
    out_send, out_recv, ring_sem, halo_sem,
):
    blk, uly = lax.axis_index("blk"), lax.axis_index("uly")
    side, z = uly // RING, lax.rem(uly, RING)
    half = blk * 2 + side
    has_prev, has_next = half > 0, half < halves - 1

    def device(h, zz):
        return (h // 2, lax.rem(h, 2) * RING + zz)

    def peer_of(offset):
        return lax.rem(z + offset, RING)

    prev_dev, next_dev = device(half - 1, z), device(half + 1, z)

    barrier = pltpu.get_barrier_semaphore()
    lead = z == LEAD

    def ring_signal(sem, offset):
        pl.semaphore_signal(
            sem, inc=1, device_id=device(half, peer_of(offset)), device_id_type=MESH
        )

    for offset in range(1, RING):

        @pl.when(peer_of(offset) != LEAD)
        def _(offset=offset):
            ring_signal(barrier, offset)

    def key_copy(i):
        src, buf = ((key_ref, k_buf), (value_ref, v_buf))[i]
        return pltpu.make_async_copy(
            src.at[:, cols_of(z, HEAD_DIM)], buf.at[rows_of(BACK + z)], recv_kv.at[i, z]
        )

    def query_copy(i):
        src, buf = ((query_ref, q_buf), (grad_ref, d_buf))[i]
        return pltpu.make_async_copy(
            src.at[:, cols_of(z, PAIR)], buf.at[rows_of(z)], recv_qd.at[i, z]
        )

    for i in range(2):
        key_copy(i).start()
        query_copy(i).start()
    own_seg = pltpu.make_async_copy(seg_ref.at[half], seg_buf.at[1], seg_sem.at[1])
    own_seg.start()
    dots_copy = pltpu.make_async_copy(dots_ref, dots_buf, seg_sem.at[2])
    dots_copy.start()

    @pl.when(has_prev)
    def _():
        pltpu.make_async_copy(seg_ref.at[half - 1], seg_buf.at[0], seg_sem.at[0]).start()

    @pl.when(jnp.logical_not(lead))
    def _():
        pl.semaphore_wait(barrier, RING - 1)
        pl.semaphore_signal(ring_sem, inc=1, device_id=device(half, LEAD), device_id_type=MESH)

    @pl.when(lead)
    def _():
        pl.semaphore_wait(ring_sem, RING - 1)

        @pl.when(has_prev)
        def _():
            pl.semaphore_signal(barrier, inc=1, device_id=prev_dev, device_id_type=MESH)

        @pl.when(has_next)
        def _():
            pl.semaphore_signal(barrier, inc=1, device_id=next_dev, device_id_type=MESH)

    def send(src, dst, send_sem, recv_sem, dev):
        return pltpu.make_async_remote_copy(
            src_ref=src, dst_ref=dst, send_sem=send_sem, recv_sem=recv_sem,
            device_id=dev, device_id_type=MESH,
        )

    def send_keys(i, offset):
        src, buf = ((key_ref, k_buf), (value_ref, v_buf))[i]
        p = peer_of(offset)
        return send(
            src.at[:, cols_of(p, HEAD_DIM)], buf.at[rows_of(BACK + z)],
            send_kv.at[i, offset], recv_kv.at[i, z], device(half, p),
        )

    def send_queries(i, offset):
        src, buf = ((query_ref, q_buf), (grad_ref, d_buf))[i]
        p = peer_of(offset)
        return send(
            src.at[:, cols_of(p, PAIR)], buf.at[rows_of(z)],
            send_qd.at[i, offset], recv_qd.at[i, z], device(half, p),
        )

    def send_dots(offset):
        p = peer_of(offset)
        return send(
            r_src.at[p, :2], r_buf.at[z, :2], send_r.at[offset], recv_r.at[z], device(half, p)
        )

    order = ORDER
    for offset in order:
        for i in range(2):
            send_keys(i, offset).start()
    dots_copy.wait()
    turned = dots_buf[...].astype(jnp.float32)
    for p in range(RING):
        r_src[p] = jnp.concatenate(
            [turned[2 * p : 2 * p + 2], jnp.zeros((6, ROWS), jnp.float32)], axis=0
        )
    r_buf[z] = r_src[z]

    for offset in order:
        send_dots(offset).start()
        for i in range(2):
            send_queries(i, offset).start()

    own_seg.wait()

    @pl.when(has_prev)
    def _():
        pltpu.make_async_copy(seg_ref.at[half], seg_buf.at[0], seg_sem.at[0]).wait()

    @pl.when(jnp.logical_not(has_prev))
    def _():
        seg_buf[0] = jnp.full((RING, ROWS), -1, jnp.int32)
        k_buf[: BACK * ROWS] = jnp.zeros((BACK * ROWS, HEAD_DIM), jnp.bfloat16)
        v_buf[: BACK * ROWS] = jnp.zeros((BACK * ROWS, HEAD_DIM), jnp.bfloat16)

    before, here = seg_buf[0], seg_buf[1]
    first = jnp.zeros((RING, ROWS), jnp.int32)
    for doc in range(16):
        below = jnp.sum(
            (before < doc).astype(jnp.int32) + (here < doc).astype(jnp.int32),
            keepdims=True,
        )
        first = jnp.where(here == doc, below, first)
    tile_of = lax.broadcasted_iota(jnp.int32, (RING, ROWS), 0)
    lane_of = lax.broadcasted_iota(jnp.int32, (RING, ROWS), 1)
    origin = (RING - BACK) * ROWS + tile_of * ROWS
    low = jnp.maximum(first - origin, lane_of + 1)
    for t in range(RING):
        low_buf[t] = jnp.broadcast_to(low[t : t + 1], (8, ROWS))

    k_acc[...] = jnp.zeros(k_acc.shape, jnp.float32)
    v_acc[...] = jnp.zeros(v_acc.shape, jnp.float32)

    def wait_keys(j):
        key_slot, value_slot = k_buf.at[rows_of(BACK + j)], v_buf.at[rows_of(BACK + j)]
        pltpu.make_async_copy(key_slot, key_slot, recv_kv.at[0, j]).wait()
        pltpu.make_async_copy(value_slot, value_slot, recv_kv.at[1, j]).wait()

    def turn_keys(index):
        kt_buf[:, rows_of(index)] = k_buf[rows_of(index)].T

    def send_halo(i, j):
        buf = (k_buf, v_buf)[i]
        return send(
            buf.at[rows_of(RING + j)], buf.at[rows_of(j)],
            halo_send.at[i, j], halo_recv.at[i, j], next_dev,
        )

    @pl.when(lead)
    def _():
        pl.semaphore_wait(barrier, has_prev.astype(jnp.int32) + has_next.astype(jnp.int32))
        for offset in range(1, RING):
            ring_signal(halo_sem, offset)

    @pl.when(jnp.logical_not(lead))
    def _():
        pl.semaphore_wait(halo_sem, 1)

    for j in range(BACK):
        wait_keys(RING - BACK + j)

        @pl.when(has_next)
        def _(j=j):
            send_halo(0, j).start()
            send_halo(1, j).start()

    def turn_late(j, carry):
        turn_keys(RING + j)
        return carry

    lax.fori_loop(0, BACK, turn_late, 0)

    def take_early(j, carry):
        wait_keys(j)
        turn_keys(BACK + j)
        return carry

    lax.fori_loop(0, RING - BACK, take_early, 0)

    @pl.when(has_prev)
    def _():
        for j in range(BACK):
            for i in range(2):
                slot = (k_buf, v_buf)[i].at[rows_of(j)]
                pltpu.make_async_copy(slot, slot, halo_recv.at[i, j]).wait()

    def turn_halo(j, carry):
        turn_keys(j)
        return carry

    lax.fori_loop(0, BACK, turn_halo, 0)

    def send_out(kind, j):
        buf, out, width = (
            (gq_buf.at[rows_of(j)], gq_ref, PAIR),
            (gkv_buf.at[0, rows_of(j)], gk_ref, HEAD_DIM),
            (gkv_buf.at[1, rows_of(j)], gv_ref, HEAD_DIM),
        )[kind]
        dst = out.at[:, cols_of(z, width)]
        remote = send(buf, dst, out_send.at[kind, j], out_recv.at[kind, z], device(half, j))
        local = pltpu.make_async_copy(buf, dst, out_recv.at[kind, z])
        return remote, local

    def start_out(kind, j):
        remote, local = send_out(kind, j)

        @pl.when(j != z)
        def _():
            remote.start()

        @pl.when(j == z)
        def _():
            local.start()

    def nt_dot(a, b):
        return lax.dot_general(
            a, b, (((1,), (1,)), ((), ())), preferred_element_type=jnp.float32
        )

    def dot(a, b):
        return jnp.dot(a, b, preferred_element_type=jnp.float32)

    def finish_keys(j, extra_key, extra_value):
        rows = rows_of(BACK + j)
        gkv_buf[0, rows_of(j)] = (
            (k_acc[rows] * SCORE_SCALE + extra_key).astype(jnp.bfloat16)
        )
        gkv_buf[1, rows_of(j)] = (v_acc[rows] + extra_value).astype(jnp.bfloat16)
        start_out(1, j)
        start_out(2, j)

    def tile(t, carry):
        for i in range(2):
            slot = (q_buf, d_buf)[i].at[rows_of(t)]
            pltpu.make_async_copy(slot, slot, recv_qd.at[i, t]).wait()

        @pl.when(t != z)
        def _():
            pltpu.make_async_copy(r_buf.at[t, :2], r_buf.at[t, :2], recv_r.at[t]).wait()

        span = rows_of(t, BACK + 1)
        queries, grads = q_buf[rows_of(t)], d_buf[rows_of(t)]
        queries = jnp.concatenate([queries[:, :HEAD_DIM], queries[:, HEAD_DIM:]], axis=0)
        grads = jnp.concatenate([grads[:, :HEAD_DIM], grads[:, HEAD_DIM:]], axis=0)
        sums = r_buf[t]
        sums = jnp.concatenate([sums[0:1], sums[1:2]], axis=1)
        least = low_buf[t][0:1]
        least = jnp.concatenate([least, least], axis=1)
        keys = k_buf[span]
        bent = jnp.tanh(nt_dot(keys, queries) * (SCORE_SCALE / SOFT_CAP))
        place = lax.broadcasted_iota(jnp.int32, (SPAN, 2 * ROWS), 0)
        column = lax.broadcasted_iota(jnp.int32, (SPAN, 2 * ROWS), 1)
        most = WINDOW + jnp.where(column < ROWS, column, column - ROWS)
        allowed = (place >= least) & (place <= most)
        weight = jnp.where(allowed, jnp.exp(SOFT_CAP * bent), 0.0)
        prob = weight * (1.0 / jnp.sum(weight, axis=0, keepdims=True))
        grad_prob = nt_dot(v_buf[span], grads)
        grad_score = (prob * (grad_prob - sums) * (1.0 - bent * bent)).astype(jnp.bfloat16)
        v_acc[span] += dot(prob.astype(jnp.bfloat16), grads)
        k_acc[span] += dot(grad_score, queries)
        turned_grad = dot(kt_buf[:, span], grad_score)
        query_grad = (turned_grad * SCORE_SCALE).T.astype(jnp.bfloat16)
        gq_buf[rows_of(t), :HEAD_DIM] = query_grad[:ROWS]
        gq_buf[rows_of(t), HEAD_DIM:] = query_grad[ROWS:]
        start_out(0, t)
        return carry

    def send_back(i, j):
        return send(
            halo_out.at[i, rows_of(j)], halo_in.at[i, rows_of(j)],
            back_send.at[i, j], back_recv.at[i, j], prev_dev,
        )

    def step_of(t):
        ahead, at = lax.rem(t - z + RING, RING), 0
        for step, offset in enumerate(order, 1):
            at = jnp.where(ahead == RING - offset, step, at)
        return at

    def done_at(first, last):
        at = step_of(first)
        for t in range(first + 1, last + 1):
            at = jnp.maximum(at, step_of(t))
        return at

    halo_done = [done_at(0, j) for j in range(BACK)]
    own_done = [done_at(j, j + BACK) for j in range(RING - BACK)]

    def one_step(step, carry):
        ahead = 0
        for at, offset in enumerate(order, 1):
            ahead = jnp.where(step == at, RING - offset, ahead)
        t = lax.rem(z + ahead, RING)
        tile(t, carry)
        for j in range(BACK):

            @pl.when((halo_done[j] == step) & has_prev)
            def _(j=j):
                rows = rows_of(j)
                halo_out[0, rows] = (k_acc[rows] * SCORE_SCALE).astype(jnp.bfloat16)
                halo_out[1, rows] = v_acc[rows].astype(jnp.bfloat16)
                send_back(0, j).start()
                send_back(1, j).start()

        return carry

    lax.fori_loop(0, RING, one_step, 0)

    def first_keys(j, carry):
        finish_keys(j, 0.0, 0.0)
        return carry

    for j in (1, 0, 2, 3):
        first_keys(j, 0)

    @pl.when(jnp.logical_not(has_next))
    def _():
        halo_in[...] = jnp.zeros(halo_in.shape, jnp.bfloat16)

    def last_keys(j, carry):
        rows = rows_of(j)

        @pl.when(has_next)
        def _():
            for i in range(2):
                slot = halo_in.at[i, rows]
                pltpu.make_async_copy(slot, slot, back_recv.at[i, j]).wait()

        finish_keys(
            RING - BACK + j,
            halo_in[0, rows].astype(jnp.float32),
            halo_in[1, rows].astype(jnp.float32),
        )
        return carry

    lax.fori_loop(0, BACK, last_keys, 0)

    for offset in order:
        for i in range(2):
            send_keys(i, offset).wait_send()
            send_queries(i, offset).wait_send()
        send_dots(offset).wait_send()

    @pl.when(has_next)
    def _():
        for j in range(BACK):
            for i in range(2):
                send_halo(i, j).wait_send()

    @pl.when(has_prev)
    def _():
        for j in range(BACK):
            for i in range(2):
                send_back(i, j).wait_send()

    def drain(j, carry):
        for kind in range(3):
            remote, _ = send_out(kind, j)

            @pl.when(j != z)
            def _(remote=remote):
                remote.wait_send()

            out, width = ((gq_ref, PAIR), (gk_ref, HEAD_DIM), (gv_ref, HEAD_DIM))[kind]
            landed = out.at[:, cols_of(j, width)]
            pltpu.make_async_copy(landed, landed, out_recv.at[kind, j]).wait()
        return carry

    lax.fori_loop(0, RING, drain, 0)


def place(*refs):
    ins, outs, bufs, get, put = refs[:3], refs[3:6], refs[6:9], refs[9], refs[10]
    parts = [(i, j) for j in range(4) for i in range(3)]

    def step(i, j, out):
        rows = pl.ds(j * (ROWS // 4), ROWS // 4)
        src, dst, sems = (bufs[i], outs[i], put) if out else (ins[i], bufs[i], get)
        return pltpu.make_async_copy(src.at[rows], dst.at[rows], sems.at[i, j])

    for i, j in parts:
        step(i, j, False).start()
    for i, j in parts:
        step(i, j, False).wait()
        step(i, j, True).start()
    for i, j in parts:
        step(i, j, True).wait()


def per_device(halves, query_in, key_in, value_in, grad_out, row_dot, segments):
    here = pl.BlockSpec(memory_space=pl.ANY)
    low, wide = jnp.bfloat16, jnp.float32
    outs = tuple(jax.ShapeDtypeStruct(a.shape, low) for a in (query_in, key_in, value_in))
    blocks = segments.reshape(halves, RING, ROWS)
    sem = pltpu.SemaphoreType.DMA
    tokens, reach = RING * ROWS, (RING + BACK) * ROWS
    flops = 5 * 2 * RING * SPAN * 2 * ROWS * HEAD_DIM
    grads = pl.pallas_call(
        functools.partial(kernel, halves),
        out_shape=outs,
        in_specs=[here] * 6,
        out_specs=(here,) * 3,
        scratch_shapes=[
            pltpu.VMEM((tokens, PAIR), low),
            pltpu.VMEM((tokens, PAIR), low),
            pltpu.VMEM((reach, HEAD_DIM), low),
            pltpu.VMEM((reach, HEAD_DIM), low),
            pltpu.VMEM((HEAD_DIM, reach), low),
            pltpu.VMEM((2 * RING, ROWS), low),
            pltpu.VMEM((RING, 8, ROWS), wide),
            pltpu.VMEM((RING, 8, ROWS), wide),
            pltpu.VMEM((2, RING, ROWS), jnp.int32),
            pltpu.VMEM((RING, 8, ROWS), jnp.int32),
            pltpu.VMEM((reach, HEAD_DIM), wide),
            pltpu.VMEM((reach, HEAD_DIM), wide),
            pltpu.VMEM((tokens, PAIR), low),
            pltpu.VMEM((2, tokens, HEAD_DIM), low),
            pltpu.VMEM((2, BACK * ROWS, HEAD_DIM), low),
            pltpu.VMEM((2, BACK * ROWS, HEAD_DIM), low),
            sem((2, RING)), sem((2, RING)), sem((RING,)),
            sem((2, RING)), sem((2, RING)), sem((RING,)), sem((3,)),
            sem((2, BACK)), sem((2, BACK)), sem((2, BACK)), sem((2, BACK)),
            sem((3, RING)), sem((3, RING)),
            pltpu.SemaphoreType.REGULAR, pltpu.SemaphoreType.REGULAR,
        ],
        compiler_params=pltpu.CompilerParams(
            collective_id=0, has_side_effects=True, vmem_limit_bytes=62 * 1024 * 1024
        ),
        cost_estimate=pl.CostEstimate(
            flops=flops, bytes_accessed=5 << 20, transcendentals=2 * RING * SPAN * 2 * ROWS
        ),
        name="window_backward",
    )(query_in, key_in, value_in, grad_out, row_dot.T, blocks)
    return pl.pallas_call(
        place,
        out_shape=outs,
        in_specs=[here] * 3,
        out_specs=(here,) * 3,
        scratch_shapes=[pltpu.VMEM(o.shape, low) for o in outs] + [sem((3, 4))] * 2,
        name="place",
    )(*grads)


def solution(mesh):
    rows = P(("blk", "uly"), None)
    halves = mesh.shape["blk"] * mesh.shape["uly"] // RING
    return jax.shard_map(
        functools.partial(per_device, halves),
        mesh=mesh,
        in_specs=(rows,) * 5 + (P(),),
        out_specs=(rows,) * 3,
        check_vma=False,
    )
```
